1024 devices in a mesh: row: 32 (over z, x_lo, core), col: 32 (over y, x_hi).
Axes of the slice: x: 8 (x_hi: 4, x_lo: 2; x = x_hi * 2 + x_lo), y: 8, z: 8, core: 2. Of those that a mesh axis runs over, the one named last changes fastest.
Arguments:
- current_block: float32 [8, 262144], P(None, ('row', 'col')), may hold values from -6 to 6
- previous_block: float32 [8, 262144], P(None, ('row', 'col')), may hold values from -6 to 6
- beta_coupling: float32 [8, 8], replicated, may hold values from -3 to 3
- diagonal: float32 [262144], P(('row', 'col')), may hold values from 0.5 to 2
- blocks: bfloat16 [32, 32, 96, 128, 128], P('row', 'col'), may hold values from -0.0546875 to 0.0546875
- near_index: int32 [32, 32, 96], P('row', 'col'), may hold values from 0 to 63
- far_index: int32 [32, 32, 96], P('row', 'col'), may hold values from 0 to 63
- counts: int32 [32, 32], P('row', 'col'), may hold values from 32 to 96, as said below
Outputs:
- residual_block: float32 [8, 262144], P(None, ('row', 'col'))
- next_block: float32 [8, 262144], P(None, ('row', 'col'))
- coefficients: float32 [3, 8, 8], replicated
The draws below stay inside these ranges and needn't reach their ends.
Inputs may be any that keep to these rules, and one draw needn't show every extreme that they name: `counts`: tiles hold different numbers of live slots; some tile in every draw has all 96 slots live.
All inputs are finite; a program needn't handle non-finite values.
Results may differ from the reference program's by a relative error of at most 0.002.
Values may be sent and summed in bfloat16 or wider, within the bound.
No kernel may reach another device: no remote copies, remote signals or barrier semaphores. Data moves between devices by JAX's collectives and lax.ppermute only.
A program may use at most 32 MiB of HBM per device.

```python
import math
import jax
import jax.numpy as jnp
from jax import lax

NV = 8
BS = 128
PB = 2
KB = 96
ROWS = 262144
N_ROW = 32
N_COL = 32


def draw_counts(key, part):
    key = jax.random.fold_in(key, 11)
    first_key, row_key, col_key = jax.random.split(key, 3)
    drawn = jax.random.randint(first_key, (N_ROW, N_COL), KB // 3, KB + 1)
    row_pick = jax.random.randint(row_key, (), 0, N_ROW)
    col_pick = jax.random.randint(col_key, (), 0, N_COL)
    return drawn.at[row_pick, col_pick].set(KB).astype(jnp.int32)


def set_ends(values, stream_key, least, top_value):
    extent = values.shape
    index_at = [jax.random.randint(jax.random.fold_in(stream_key, axis), (), 0, extent[axis]) for axis in range(len(extent))]
    values = values.at[tuple(index_at)].set(least)
    longest = extent.index(max(extent))
    index_at[longest] = (index_at[longest] + 1) % extent[longest]
    return values.at[tuple(index_at)].set(top_value)


def block_levels(key, shape, shards, smallest, top_value):
    factor_of = 1.0
    for axis_at, blocks in shards:
        steps = jax.random.uniform(jax.random.fold_in(jax.random.fold_in(key, 6), axis_at), (blocks,), jnp.float32, smallest / len(shards), top_value / len(shards))
        factor_of = factor_of * jnp.repeat(jnp.exp(steps), shape[axis_at] // blocks).reshape((-1,) + (1,) * (len(shape) - 1 - axis_at))
    return factor_of


def noise(stream_key, shape, scale, most, shards=(), held_as=jnp.bfloat16):
    result = scale * jax.random.normal(stream_key, shape, jnp.float32)
    if shards:
        result = result * block_levels(stream_key, shape, shards, -0.22, 0.18)
    return jnp.clip(result, -most, most).astype(held_as)


def setup_inputs(seed: int = 0) -> dict:
    seeds = jax.random.split(jax.random.key(seed), 9)
    current_block = noise(seeds[0], (NV, ROWS), 1.0, 6.0, ((1, 1024),), jnp.float32)
    previous_block = noise(seeds[1], (NV, ROWS), 1.0, 6.0, ((1, 1024),), jnp.float32)
    beta_coupling = noise(seeds[2], (NV, NV), 0.5, 3.0, (), jnp.float32)
    diagonal = jnp.clip(jnp.exp(math.log(2.0) - 1.3862944 * jax.random.uniform(seeds[3], (ROWS,), jnp.float32) ** block_levels(seeds[3], (ROWS,), ((0, 1024),), -0.2, 0.2)), 0.5, 2.0)
    blocks = noise(seeds[4], (N_ROW, N_COL, KB, BS, BS), (2 * KB * BS // PB) ** -0.5, 0.0546875, ((0, 32), (1, 32)))
    near_index = set_ends(jax.random.randint(seeds[5], (N_ROW, N_COL, KB), 0, N_COL * PB), jax.random.fold_in(seeds[5], 1), 0, (N_COL * PB) - 1).astype(jnp.int32)
    far_index = set_ends(jax.random.randint(seeds[6], (N_ROW, N_COL, KB), 0, N_ROW * PB), jax.random.fold_in(seeds[6], 1), 0, (N_ROW * PB) - 1).astype(jnp.int32)
    counts = draw_counts(jax.random.fold_in(seeds[8], 71), 0)
    return dict(current_block=current_block, previous_block=previous_block, beta_coupling=beta_coupling, diagonal=diagonal, blocks=blocks, near_index=near_index, far_index=far_index, counts=counts)


def apply_matrix(vectors, blocks, near_index, far_index, counts, diagonal):
    near_total = N_COL * PB
    far_total = N_ROW * PB
    rounded = vectors.astype(jnp.bfloat16)
    vector_grid = rounded.reshape(NV, N_ROW, N_COL, PB, BS)
    column_segments = jnp.transpose(vector_grid, (2, 0, 1, 3, 4)).reshape(N_COL, NV, far_total, BS)
    slot_range = jnp.arange(KB)

    def one_row(running, row_index):
        row_segment = lax.dynamic_index_in_dim(vector_grid, row_index, 1, keepdims=False).reshape(NV, near_total, BS)
        row_blocks = lax.dynamic_index_in_dim(blocks, row_index, 0, keepdims=False)
        row_near = lax.dynamic_index_in_dim(near_index, row_index, 0, keepdims=False)
        row_far = lax.dynamic_index_in_dim(far_index, row_index, 0, keepdims=False)
        row_counts = lax.dynamic_index_in_dim(counts, row_index, 0, keepdims=False)

        def one_tile(block_list, near_list, far_list, live_count, column_segment):
            live_mask = (slot_range < live_count).astype(jnp.float32)
            from_far = jnp.take(column_segment, far_list, axis=1).astype(jnp.float32)
            from_near = jnp.take(row_segment, near_list, axis=1).astype(jnp.float32)
            block_float = block_list.astype(jnp.float32)
            to_near = jnp.einsum('vkj,kij->vki', from_far, block_float)
            to_far = jnp.einsum('vki,kij->vkj', from_near, block_float)
            pick_near = (near_list[:, None] == jnp.arange(near_total)[None, :]).astype(jnp.float32) * live_mask[:, None]
            pick_far = (far_list[:, None] == jnp.arange(far_total)[None, :]).astype(jnp.float32) * live_mask[:, None]
            near_part = jnp.einsum('vki,kn->vni', to_near, pick_near, precision=lax.Precision.HIGHEST)
            far_part = jnp.einsum('vkj,kn->vnj', to_far, pick_far, precision=lax.Precision.HIGHEST)
            return (near_part, far_part)
        near_parts, far_parts = jax.vmap(one_tile)(row_blocks, row_near, row_far, row_counts, column_segments)
        return (running + far_parts, jnp.sum(near_parts, axis=0))
    start = jnp.zeros((N_COL, NV, far_total, BS), jnp.float32)
    column_totals, row_totals = lax.scan(one_row, start, jnp.arange(N_ROW))
    from_rows = jnp.transpose(row_totals, (1, 0, 2, 3)).reshape(NV, ROWS)
    from_columns = jnp.transpose(column_totals.reshape(N_COL, NV, N_ROW, PB, BS), (1, 2, 0, 3, 4)).reshape(NV, ROWS)
    return from_rows + from_columns + diagonal[None, :] * vectors

def inner_products(left, right):
    return jnp.dot(left, right.T, precision=lax.Precision.HIGHEST)

def reference(current_block, previous_block, beta_coupling, diagonal, blocks, near_index, far_index, counts):
    product = apply_matrix(current_block, blocks, near_index, far_index, counts, diagonal)
    product = product - jnp.dot(beta_coupling, previous_block, precision=lax.Precision.HIGHEST)
    alpha_one = inner_products(current_block, product) / ROWS
    adjusted = product - jnp.dot(alpha_one.T, current_block, precision=lax.Precision.HIGHEST)
    moment = inner_products(adjusted, adjusted) / ROWS
    factor = jnp.linalg.cholesky(moment)
    next_block = lax.linalg.triangular_solve(factor, adjusted, left_side=True, lower=True)
    second = apply_matrix(next_block, blocks, near_index, far_index, counts, diagonal)
    second = second - jnp.dot(factor.T, current_block, precision=lax.Precision.HIGHEST)
    alpha_two = inner_products(next_block, second) / ROWS
    residual_block = second - jnp.dot(alpha_two.T, next_block, precision=lax.Precision.HIGHEST)
    return (residual_block, next_block, jnp.stack([alpha_one, factor, alpha_two]))
```

```python
import jax
import jax.numpy as jnp
from jax import lax
from jax.sharding import PartitionSpec as P

HIGHEST = lax.Precision.HIGHEST


def exchange(chunks, axis):
    return lax.all_to_all(chunks, axis, split_axis=0, concat_axis=0, tiled=True)


def gather_from(chunk, axis):
    size = lax.axis_size(axis)
    return exchange(jnp.broadcast_to(chunk[None], (size,) + chunk.shape), axis)


def inner(left, right):
    return jnp.einsum("tvi,twi->vw", left, right, precision=HIGHEST)


def mix(matrix, vectors):
    return jnp.einsum("uv,tvi->tui", matrix, vectors, precision=HIGHEST)


def dot(left, right):
    return jnp.dot(left, right, precision=HIGHEST)


def on_device(
    current_block, previous_block, beta_coupling, diagonal, blocks, near_index, far_index, counts
):
    tile_blocks = blocks[0, 0]
    near_list = near_index[0, 0]
    far_list = far_index[0, 0]
    live_count = counts[0, 0]
    nv, share = current_block.shape
    width = tile_blocks.shape[-1]
    pb = share // width
    slots = tile_blocks.shape[0]
    n_row, n_col = lax.axis_size("row"), lax.axis_size("col")
    rows_total = share * n_row * n_col
    live_mask = (jnp.arange(slots) < live_count).astype(jnp.float32)
    near_total, far_total = n_col * pb, n_row * pb
    pick_near = (near_list[:, None] == jnp.arange(near_total)[None, :]).astype(
        jnp.float32
    ) * live_mask[:, None]
    pick_far = (far_list[:, None] == jnp.arange(far_total)[None, :]).astype(
        jnp.float32
    ) * live_mask[:, None]

    def local_form(vectors):
        return vectors.reshape(nv, pb, width).transpose(1, 0, 2)

    def tile_products(near_vectors, far_vectors):
        from_far = jnp.take(far_vectors, far_list, axis=0)
        from_near = jnp.take(near_vectors, near_list, axis=0)
        to_near = jnp.einsum(
            "kvj,kij->kvi", from_far, tile_blocks, preferred_element_type=jnp.float32
        )
        to_far = jnp.einsum(
            "kvi,kij->kvj", from_near, tile_blocks, preferred_element_type=jnp.float32
        )
        return to_near, to_far

    def place(products, pick):
        return jnp.einsum("kvi,kn->nvi", products, pick, precision=HIGHEST)

    current = local_form(current_block)
    previous = local_form(previous_block)
    diag = diagonal.reshape(pb, 1, width)

    rounded = current.astype(jnp.bfloat16).reshape(pb * nv, width)
    near_vectors = gather_from(rounded, "col").reshape(near_total, nv, width)
    far_vectors = gather_from(rounded, "row").reshape(far_total, nv, width)
    to_near, to_far = tile_products(near_vectors, far_vectors)
    near_part = place(to_near, pick_near).reshape(n_col, pb, nv, width)
    far_part = place(to_far, pick_far).reshape(n_row, pb, nv, width)
    off_diagonal = exchange(near_part, "col").sum(0) + exchange(far_part, "row").sum(0)
    applied = off_diagonal + diag * current
    product = applied - mix(beta_coupling, previous)

    grams = jnp.concatenate(
        [
            inner(current, product),
            inner(product, product),
            inner(current, current),
            inner(product, applied),
            inner(current, applied),
        ],
        axis=1,
    )
    grams = jnp.pad(grams, ((0, 0), (0, width - grams.shape[1])))
    got = gather_from(jnp.concatenate([product, grams[None]]), "col")
    grams = got[:, pb].sum(0)
    near_product = got[:, :pb].reshape(near_total, nv, width)
    got = gather_from(jnp.concatenate([product, grams[None]]), "row")
    grams = got[:, pb].sum(0)
    far_product = got[:, :pb].reshape(far_total, nv, width)

    def split(vectors):
        high = vectors.astype(jnp.bfloat16)
        low = (vectors - high.astype(jnp.float32)).astype(jnp.bfloat16)
        return jnp.concatenate([high, low], axis=1)

    to_near, to_far = tile_products(split(near_product), split(far_product))
    to_near = to_near[:, :nv] + to_near[:, nv:]
    to_far = to_far[:, :nv] + to_far[:, nv:]
    near_part = place(to_near, pick_near)
    far_part = place(to_far, pick_far).reshape(n_row, pb, nv, width)
    quadratic = inner(near_product, near_part)
    quadratic = quadratic + quadratic.T + inner(product, diag * product)
    quadratic = jnp.pad(quadratic, ((0, 0), (0, width - nv)))
    near_part = jnp.concatenate(
        [
            near_part.reshape(n_col, pb, nv, width),
            jnp.broadcast_to(quadratic, (n_col, 1, nv, width)),
        ],
        axis=1,
    )
    near_got = exchange(near_part, "col").sum(0)
    far_part = jnp.concatenate(
        [far_part, jnp.broadcast_to(near_got[pb], (n_row, 1, nv, width))], axis=1
    )
    far_got = exchange(far_part, "row").sum(0)
    applied_product = near_got[:pb] + far_got[:pb] + diag * product
    pw = far_got[pb, :, :nv]

    cp, pp, cc, pu, cu = (grams[:, i * nv : (i + 1) * nv] for i in range(5))
    alpha_one = cp / rows_total
    at = alpha_one.T
    moment = (pp - dot(at, cp) - dot(cp.T, alpha_one) + dot(dot(at, cc), alpha_one)) / rows_total
    factor = jnp.linalg.cholesky(moment)
    inverse = lax.linalg.triangular_solve(
        factor, jnp.eye(nv, dtype=jnp.float32), left_side=True, lower=True
    )
    next_block = mix(inverse, product - mix(at, current))
    second = mix(inverse, applied_product - mix(at, applied)) - mix(factor.T, current)
    half = dot(pu, alpha_one)
    vhv = dot(dot(inverse, pw - half - half.T + dot(dot(at, cu), alpha_one)), inverse.T)
    vc = dot(inverse, cp.T - dot(at, cc))
    alpha_two = (vhv - dot(vc, factor)) / rows_total
    residual = second - mix(alpha_two.T, next_block)

    def whole_form(vectors):
        return vectors.transpose(1, 0, 2).reshape(nv, share)

    return (
        whole_form(residual),
        whole_form(next_block),
        jnp.stack([alpha_one, factor, alpha_two]),
    )


def solution(mesh):
    return jax.shard_map(
        on_device,
        mesh=mesh,
        in_specs=(
            P(None, ("row", "col")),
            P(None, ("row", "col")),
            P(),
            P(("row", "col")),
            P("row", "col", None, None, None),
            P("row", "col", None),
            P("row", "col", None),
            P("row", "col"),
        ),
        out_specs=(P(None, ("row", "col")), P(None, ("row", "col")), P()),
        check_vma=False,
    )
```

```python
import functools

import jax
import jax.numpy as jnp
from jax import lax
from jax.experimental import pallas as pl
from jax.experimental.pallas import tpu as pltpu
from jax.sharding import PartitionSpec as P

HIGHEST = lax.Precision.HIGHEST
F32 = jnp.float32
BF16 = jnp.bfloat16
SHIFT = 1.25
VMEM = pl.BlockSpec(memory_space=pltpu.VMEM)
SMEM = pl.BlockSpec(memory_space=pltpu.SMEM)
PARAMS = pltpu.CompilerParams(vmem_limit_bytes=24 * 1024 * 1024)


def exchange(chunks, axis):
    return lax.all_to_all(chunks, axis, split_axis=0, concat_axis=0, tiled=True)


def call(kernel, out_shape, in_specs, scratch=()):
    many = isinstance(out_shape, (list, tuple))
    return pl.pallas_call(
        kernel,
        out_shape=out_shape,
        in_specs=in_specs,
        out_specs=tuple(VMEM for _ in out_shape) if many else VMEM,
        scratch_shapes=list(scratch),
        compiler_params=PARAMS,
    )


def shape_of(shape, dtype=F32):
    return jax.ShapeDtypeStruct(shape, dtype)


def pieces(ref):
    width = ref.shape[-1] // 2
    return [ref[:, :width], ref[:, width:]]


def contract_last(left, right):
    return lax.dot_general(
        left, right, (((1,), (1,)), ((), ())), precision=HIGHEST, preferred_element_type=F32
    )


def small_dot(left, right):
    total = left[:, 0:1] * right[0:1, :]
    for k in range(1, right.shape[0]):
        total = total + left[:, k : k + 1] * right[k : k + 1, :]
    return total


def identity(size):
    rows = lax.broadcasted_iota(jnp.int32, (size, size), 0)
    return (rows == lax.broadcasted_iota(jnp.int32, (size, size), 1)).astype(F32)


def rounded_kernel(vectors_ref, out_ref):
    chunk = jnp.concatenate(pieces(vectors_ref), axis=0).astype(BF16)
    out_ref[...] = jnp.broadcast_to(chunk[None], out_ref.shape)


def multiply_slots(src_ref, vectors_ref, blocks_ref, products_ref, over_columns):
    dims = (((1,), (1 if over_columns else 0,)), ((), ()))
    for k in range(blocks_ref.shape[0]):
        pair = vectors_ref[lax.shift_right_logical(src_ref[k], 1)]
        products_ref[k] = lax.dot_general(
            pair, blocks_ref[k], dims, preferred_element_type=F32
        )


def place_slots(src_ref, dst_ref, count_ref, products_ref, add):
    nv = products_ref.shape[1] // 2

    def one_slot(k, carry):
        half = pl.multiple_of((src_ref[k] & 1) * nv, nv)
        add(dst_ref[k], products_ref[k, pl.ds(half, nv), :])
        return carry

    lax.fori_loop(0, count_ref[0], one_slot, 0)


def products_kernel(
    over_columns, src_ref, dst_ref, count_ref, vectors_ref, blocks_ref, out_ref, products_ref
):
    multiply_slots(src_ref, vectors_ref, blocks_ref, products_ref, over_columns)
    out_ref[...] = jnp.zeros_like(out_ref)

    def add(block, values):
        out_ref[block >> 1, block & 1] += values

    place_slots(src_ref, dst_ref, count_ref, products_ref, add)


def near_kernel(
    src_ref,
    dst_ref,
    count_ref,
    vectors_ref,
    near_ref,
    blocks_ref,
    shifted_ref,
    diagonal_ref,
    grams_ref,
    out_ref,
    products_ref,
):
    products_kernel(
        True, src_ref, dst_ref, count_ref, vectors_ref, blocks_ref, out_ref, products_ref
    )
    nv, width = out_ref.shape[2:]
    total = jnp.zeros((2 * nv, 2 * nv), F32)
    for n in range(out_ref.shape[0]):
        pair = jnp.concatenate([out_ref[n, 0], out_ref[n, 1]], axis=0)
        total = total + contract_last(pair, near_ref[n].astype(F32))
    quadratic = total[:nv, :nv] + total[nv:, nv:]
    quadratic = quadratic + contract_last(identity(nv), quadratic)
    for vectors, diag in zip(pieces(shifted_ref), pieces(diagonal_ref)):
        quadratic = quadratic + contract_last(vectors, diag * vectors)
    used = 9 * nv
    extra = jnp.concatenate(
        [grams_ref[:, :used], quadratic, jnp.zeros((nv, width - used - nv), F32)], axis=1
    )
    for n in range(out_ref.shape[0]):
        out_ref[n, 2] = extra


def middle_kernel(
    near_ref,
    far_ref,
    current_ref,
    previous_ref,
    beta_ref,
    diagonal_ref,
    applied_ref,
    shifted_ref,
    payload_ref,
    grams_ref,
):
    nv, width = near_ref.shape[2:]
    beta = beta_ref[...]
    total = jnp.zeros((3 * nv, 3 * nv), F32)
    halves = []
    for t in range(2):
        part = slice(t * width, (t + 1) * width)
        current = current_ref[:, part]
        off_diagonal = jnp.sum(near_ref[:, t], axis=0) + jnp.sum(far_ref[:, t], axis=0)
        applied = off_diagonal + diagonal_ref[:, part] * current
        shifted = applied - small_dot(beta, previous_ref[:, part]) - SHIFT * current
        applied_ref[:, part] = applied
        shifted_ref[:, part] = shifted
        stack = jnp.concatenate([current, shifted, applied], axis=0)
        total = total + contract_last(stack, stack)
        halves.append(shifted)
    chunk = jnp.concatenate(halves, axis=0).astype(BF16)
    payload_ref[...] = jnp.broadcast_to(chunk[None], payload_ref.shape)
    grams_ref[...] = jnp.concatenate(
        [total[:nv], total[nv : 2 * nv], total[2 * nv :], jnp.zeros((nv, width - 9 * nv), F32)],
        axis=1,
    )


def forward_kernel(near_ref, far_ref, sum_ref, out_ref):
    total = jnp.sum(near_ref[...], axis=0)
    sum_ref[...] = total[:2]
    out_ref[:, :2] = far_ref[...]
    out_ref[:, 2] = jnp.broadcast_to(total[2][None], out_ref[:, 2].shape)


def last_kernel(
    rows_total,
    near_ref,
    far_ref,
    current_ref,
    shifted_ref,
    applied_ref,
    diagonal_ref,
    residual_ref,
    next_ref,
    coefficients_ref,
):
    nv, width = near_ref.shape[1:]
    received = jnp.sum(far_ref[...], axis=0)
    extra = received[2]
    gram = lambda i: extra[:, i * nv : (i + 1) * nv]
    cc, cx, cu, xc, xx, xu, _, ux, _, xw = (gram(i) for i in range(10))
    eye = identity(nv)
    scale = 1.0 / rows_total
    alpha_one = (cx + SHIFT * cc) * scale
    alpha = alpha_one - SHIFT * eye
    alpha_t = (xc + SHIFT * cc) * scale - SHIFT * eye
    adjusted_c = xc - small_dot(alpha_t, cc)
    work = (xx - small_dot(alpha_t, cx) - small_dot(adjusted_c, alpha)) * scale
    rows = lax.broadcasted_iota(jnp.int32, (nv, nv), 0)
    columns = lax.broadcasted_iota(jnp.int32, (nv, nv), 1)
    factor = jnp.zeros((nv, nv), F32)
    factor_t = jnp.zeros((nv, nv), F32)
    inverse = eye
    for j in range(nv):
        root = lax.rsqrt(work[j : j + 1, j : j + 1])
        column = jnp.where(rows[:, :1] >= j, work[:, j : j + 1] * root, 0.0)
        row = jnp.where(columns[:1] >= j, work[j : j + 1, :] * root, 0.0)
        factor = jnp.where(columns == j, column, factor)
        factor_t = jnp.where(rows == j, row, factor_t)
        work = work - column * row
        done = inverse[j : j + 1, :] * root
        below = jnp.where(rows[:, :1] > j, column, 0.0)
        inverse = jnp.where(rows == j, done, inverse - below * done)
    z = (
        xw
        - small_dot(xu, alpha)
        - small_dot(alpha_t, ux)
        + small_dot(small_dot(alpha_t, cu), alpha)
    )
    alpha_two = contract_last(small_dot(inverse, z), inverse)
    alpha_two = (alpha_two - small_dot(small_dot(inverse, adjusted_c), factor)) * scale
    alpha_two_t = contract_last(eye, alpha_two)
    for t in range(2):
        part = slice(t * width, (t + 1) * width)
        current = current_ref[:, part]
        shifted = shifted_ref[:, part]
        applied_shifted = near_ref[t] + received[t] + diagonal_ref[:, part] * shifted
        following = small_dot(inverse, shifted - small_dot(alpha_t, current))
        second = small_dot(inverse, applied_shifted - small_dot(alpha_t, applied_ref[:, part]))
        second = second - small_dot(factor_t, current)
        next_ref[:, part] = following
        residual_ref[:, part] = second - small_dot(alpha_two_t, following)
    coefficients_ref[0] = alpha_one
    coefficients_ref[1] = factor
    coefficients_ref[2] = alpha_two


def on_device(
    current_block, previous_block, beta_coupling, diagonal, blocks, near_index, far_index, counts
):
    tile_blocks = blocks[0, 0]
    near_list = near_index[0, 0]
    far_list = far_index[0, 0]
    live_count = counts[0]
    nv, share = current_block.shape
    slots, width = tile_blocks.shape[:2]
    n_row, n_col = lax.axis_size("row"), lax.axis_size("col")
    rows_total = share * n_row * n_col
    diag = diagonal.reshape(1, share)
    vector = shape_of((nv, share))

    def products(over_columns, src, dst, vectors, peers):
        return call(
            functools.partial(products_kernel, over_columns),
            shape_of((peers, 2, nv, width)),
            [SMEM] * 3 + [VMEM] * 2,
            [pltpu.VMEM((slots, 2 * nv, width), F32)],
        )(src, dst, live_count, vectors, tile_blocks)

    chunks = call(rounded_kernel, shape_of((n_col, 2 * nv, width), BF16), [VMEM])(current_block)
    near_vectors = exchange(chunks, "col")
    far_vectors = exchange(chunks, "row")
    far_part = products(False, near_list, far_list, near_vectors, n_row)
    far_got = exchange(far_part, "row")
    near_part = products(True, far_list, near_list, far_vectors, n_col)
    near_got = exchange(near_part, "col")
    applied, shifted, chunks, grams = call(
        middle_kernel,
        (vector, vector, shape_of((n_col, 2 * nv, width), BF16), shape_of((nv, width))),
        [VMEM] * 6,
    )(near_got, far_got, current_block, previous_block, beta_coupling, diag)

    far_vectors = exchange(chunks, "row")
    near_vectors = exchange(chunks, "col")
    near_part = call(
        near_kernel,
        shape_of((n_col, 3, nv, width)),
        [SMEM] * 3 + [VMEM] * 6,
        [pltpu.VMEM((slots, 2 * nv, width), F32)],
    )(
        far_list,
        near_list,
        live_count,
        far_vectors,
        near_vectors,
        tile_blocks,
        shifted,
        diag,
        grams,
    )
    near_got = exchange(near_part, "col")
    far_part = products(False, near_list, far_list, near_vectors, n_row)
    near_sum, far_part = call(
        forward_kernel, (shape_of((2, nv, width)), shape_of((n_row, 3, nv, width))), [VMEM] * 2
    )(near_got, far_part)
    far_got = exchange(far_part, "row")
    return call(
        functools.partial(last_kernel, rows_total),
        (vector, vector, shape_of((3, nv, nv))),
        [VMEM] * 6,
    )(near_sum, far_got, current_block, shifted, applied, diag)


def solution(mesh):
    return jax.shard_map(
        on_device,
        mesh=mesh,
        in_specs=(
            P(None, ("row", "col")),
            P(None, ("row", "col")),
            P(),
            P(("row", "col")),
            P("row", "col", None, None, None),
            P("row", "col", None),
            P("row", "col", None),
            P("row", "col"),
        ),
        out_specs=(P(None, ("row", "col")), P(None, ("row", "col")), P()),
        check_vma=False,
    )
```

```python
import functools

import jax
import jax.numpy as jnp
from jax import lax
from jax.experimental import pallas as pl
from jax.experimental.pallas import tpu as pltpu
from jax.sharding import PartitionSpec as P

HIGHEST = lax.Precision.HIGHEST
F32 = jnp.float32
BF16 = jnp.bfloat16
SHIFT = 1.25
VMEM = pl.BlockSpec(memory_space=pltpu.VMEM)
SMEM = pl.BlockSpec(memory_space=pltpu.SMEM)
PARAMS = pltpu.CompilerParams(vmem_limit_bytes=24 * 1024 * 1024)


def exchange(chunks, axis):
    return lax.all_to_all(chunks, axis, split_axis=0, concat_axis=0, tiled=True)


def call(kernel, out_shape, in_specs, scratch=()):
    many = isinstance(out_shape, (list, tuple))
    return pl.pallas_call(
        kernel,
        out_shape=out_shape,
        in_specs=in_specs,
        out_specs=tuple(VMEM for _ in out_shape) if many else VMEM,
        scratch_shapes=list(scratch),
        compiler_params=PARAMS,
    )


def shape_of(shape, dtype=F32):
    return jax.ShapeDtypeStruct(shape, dtype)


def pieces(ref):
    width = ref.shape[-1] // 2
    return [ref[:, :width], ref[:, width:]]


def contract_last(left, right):
    return lax.dot_general(
        left, right, (((1,), (1,)), ((), ())), precision=HIGHEST, preferred_element_type=F32
    )


def small_dot(left, right):
    total = left[:, 0:1] * right[0:1, :]
    for k in range(1, right.shape[0]):
        total = total + left[:, k : k + 1] * right[k : k + 1, :]
    return total


def identity(size):
    rows = lax.broadcasted_iota(jnp.int32, (size, size), 0)
    return (rows == lax.broadcasted_iota(jnp.int32, (size, size), 1)).astype(F32)


def split_three(values):
    high = values.astype(BF16)
    rest = values - high.astype(F32)
    middle = rest.astype(BF16)
    return high, middle, (rest - middle.astype(F32)).astype(BF16)


def pack_extra(values, shape):
    parts = [piece[:, :80].astype(F32) for piece in split_three(values)]
    top = jnp.concatenate([parts[0], parts[1][:, :48]], axis=1)
    zeros = jnp.zeros((shape[0] // 2, shape[1] - 32 - 80), F32)
    bottom = jnp.concatenate([parts[2], parts[1][:, 48:80], zeros], axis=1)
    return jnp.concatenate([top, bottom], axis=0).astype(BF16)


def unpack_extra(total):
    nv = total.shape[0] // 2
    top, bottom = total[:nv], total[nv:]
    middle = jnp.concatenate([top[:, 80:128], bottom[:, 80:112]], axis=1)
    return top[:, :80] + (middle + bottom[:, :80])


def rounded_kernel(vectors_ref, out_ref):
    chunk = jnp.concatenate(pieces(vectors_ref), axis=0).astype(BF16)
    out_ref[...] = jnp.broadcast_to(chunk[None], out_ref.shape)


def pack_kernel(current_ref, previous_ref, beta_ref, diagonal_ref, out_ref):
    nv = current_ref.shape[0]
    out_ref[:nv] = current_ref[...]
    out_ref[nv : 2 * nv] = small_dot(beta_ref[...], previous_ref[...])
    out_ref[2 * nv :] = jnp.broadcast_to(diagonal_ref[...], (nv, out_ref.shape[1]))


def multiply_slots(lists_ref, src, vectors_ref, blocks_ref, products_ref, over_columns):
    dims = (((1,), (1 if over_columns else 0,)), ((), ()))
    for k in range(blocks_ref.shape[0]):
        pair = vectors_ref[lax.shift_right_logical(lists_ref[src + k], 1)]
        products_ref[k] = lax.dot_general(
            pair, blocks_ref[k], dims, preferred_element_type=F32
        )


def products_into(over_columns, lists_ref, vectors_ref, blocks_ref, out_ref, products_ref):
    slots = blocks_ref.shape[0]
    src, dst = (slots, 0) if over_columns else (0, slots)
    nv = out_ref.shape[2]
    multiply_slots(lists_ref, src, vectors_ref, blocks_ref, products_ref, over_columns)
    out_ref[...] = jnp.zeros_like(out_ref)

    def one_slot(k, carry):
        half = pl.multiple_of((lists_ref[src + k] & 1) * nv, nv)
        block = lists_ref[dst + k]
        out_ref[lax.shift_right_logical(block, 1), block & 1] += products_ref[
            k, pl.ds(half, nv), :
        ]
        return carry

    lax.fori_loop(0, lists_ref[2 * slots], one_slot, 0)


def pair_of(ref, n):
    return jnp.concatenate([ref[n, 0], ref[n, 1]], axis=0)


def rounded_products_kernel(
    over_columns, lists_ref, vectors_ref, blocks_ref, out_ref, products_ref, sums_ref
):
    products_into(over_columns, lists_ref, vectors_ref, blocks_ref, sums_ref, products_ref)
    for n in range(out_ref.shape[0]):
        out_ref[n] = pair_of(sums_ref, n).astype(BF16)


def near_kernel(
    lists_ref, vectors_ref, near_ref, blocks_ref, state_ref, out_ref, products_ref, sums_ref
):
    products_into(True, lists_ref, vectors_ref, blocks_ref, sums_ref, products_ref)
    nv, width = sums_ref.shape[2:]
    total = jnp.zeros((4 * nv, 2 * nv), F32)
    for n in range(out_ref.shape[0]):
        pair = pair_of(sums_ref, n)
        high = pair.astype(BF16)
        low = (pair - high.astype(F32)).astype(BF16)
        out_ref[n, 0] = high
        total = total + lax.dot_general(
            jnp.concatenate([high, low], axis=0),
            near_ref[n],
            (((1,), (1,)), ((), ())),
            preferred_element_type=F32,
        )
    total = total[: 2 * nv] + total[2 * nv :]
    quadratic = total[:nv, :nv] + total[nv:, nv:]
    quadratic = quadratic + contract_last(identity(nv), quadratic)
    shifted = state_ref[nv : 2 * nv]
    quadratic = quadratic + contract_last(shifted, state_ref[3 * nv : 4 * nv] * shifted)
    used = 9 * nv
    extra = jnp.concatenate(
        [
            state_ref[4 * nv :, :used],
            quadratic,
            jnp.zeros((nv, width - used - nv), F32),
        ],
        axis=1,
    )
    packed = pack_extra(extra, (2 * nv, width))
    for n in range(out_ref.shape[0]):
        out_ref[n, 1] = packed


def middle_kernel(near_ref, far_ref, constants_ref, state_ref, payload_ref):
    nv, width = near_ref.shape[2:]
    total = jnp.zeros((3 * nv, 3 * nv), F32)
    halves = []
    for t in range(2):
        part = slice(t * width, (t + 1) * width)
        current = constants_ref[:nv, part]
        diag = constants_ref[2 * nv :, part]
        off_diagonal = jnp.sum(near_ref[:, t], axis=0) + jnp.sum(far_ref[:, t], axis=0)
        applied = off_diagonal + diag * current
        shifted = applied - constants_ref[nv : 2 * nv, part] - SHIFT * current
        stack = jnp.concatenate([current, shifted, applied], axis=0)
        state_ref[: 3 * nv, part] = stack
        state_ref[3 * nv : 4 * nv, part] = diag
        total = total + contract_last(stack, stack)
        halves.append(shifted)
    chunk = jnp.concatenate(halves, axis=0).astype(BF16)
    payload_ref[...] = jnp.broadcast_to(chunk[None], payload_ref.shape)
    state_ref[4 * nv :] = jnp.concatenate(
        [
            total[:nv],
            total[nv : 2 * nv],
            total[2 * nv :],
            jnp.zeros((nv, 2 * width - 9 * nv), F32),
        ],
        axis=1,
    )


def forward_kernel(near_ref, far_ref, sum_ref, out_ref):
    nv, width = sum_ref.shape[1:]
    total = jnp.sum(near_ref[:, 0].astype(F32), axis=0)
    sum_ref[0] = total[:nv]
    sum_ref[1] = total[nv:]
    extra = unpack_extra(jnp.sum(near_ref[:, 1].astype(F32), axis=0))
    extra = jnp.concatenate([extra, jnp.zeros((nv, width - 80), F32)], axis=1)
    out_ref[:, 0] = far_ref[...]
    out_ref[:, 1] = jnp.broadcast_to(
        pack_extra(extra, (2 * nv, width))[None], out_ref[:, 1].shape
    )


def last_kernel(
    rows_total, near_ref, far_ref, state_ref, residual_ref, next_ref, coefficients_ref
):
    nv, width = near_ref.shape[1:]
    far_sum = jnp.sum(far_ref[:, 0].astype(F32), axis=0)
    extra = unpack_extra(jnp.sum(far_ref[:, 1].astype(F32), axis=0))
    gram = lambda i: extra[:, i * nv : (i + 1) * nv]
    cc, cx, cu, xc, xx, xu, _, ux, _, xw = (gram(i) for i in range(10))
    eye = identity(nv)
    scale = 1.0 / rows_total
    alpha_one = (cx + SHIFT * cc) * scale
    alpha = alpha_one - SHIFT * eye
    alpha_t = (xc + SHIFT * cc) * scale - SHIFT * eye
    adjusted_c = xc - small_dot(alpha_t, cc)
    work = (xx - small_dot(alpha_t, cx) - small_dot(adjusted_c, alpha)) * scale
    rows = lax.broadcasted_iota(jnp.int32, (nv, nv), 0)
    columns = lax.broadcasted_iota(jnp.int32, (nv, nv), 1)
    factor = jnp.zeros((nv, nv), F32)
    factor_t = jnp.zeros((nv, nv), F32)
    inverse = eye
    for j in range(nv):
        root = lax.rsqrt(work[j : j + 1, j : j + 1])
        column = jnp.where(rows[:, :1] >= j, work[:, j : j + 1] * root, 0.0)
        row = jnp.where(columns[:1] >= j, work[j : j + 1, :] * root, 0.0)
        factor = jnp.where(columns == j, column, factor)
        factor_t = jnp.where(rows == j, row, factor_t)
        work = work - column * row
        done = inverse[j : j + 1, :] * root
        below = jnp.where(rows[:, :1] > j, column, 0.0)
        inverse = jnp.where(rows == j, done, inverse - below * done)
    z = (
        xw
        - small_dot(xu, alpha)
        - small_dot(alpha_t, ux)
        + small_dot(small_dot(alpha_t, cu), alpha)
    )
    alpha_two = contract_last(small_dot(inverse, z), inverse)
    alpha_two = (alpha_two - small_dot(small_dot(inverse, adjusted_c), factor)) * scale
    alpha_two_t = contract_last(eye, alpha_two)
    for t in range(2):
        part = slice(t * width, (t + 1) * width)
        current = state_ref[:nv, part]
        shifted = state_ref[nv : 2 * nv, part]
        applied = state_ref[2 * nv : 3 * nv, part]
        applied_shifted = near_ref[t] + far_sum[t * nv : (t + 1) * nv]
        applied_shifted = applied_shifted + state_ref[3 * nv : 4 * nv, part] * shifted
        following = small_dot(inverse, shifted - small_dot(alpha_t, current))
        second = small_dot(inverse, applied_shifted - small_dot(alpha_t, applied))
        second = second - small_dot(factor_t, current)
        next_ref[:, part] = following
        residual_ref[:, part] = second - small_dot(alpha_two_t, following)
    coefficients_ref[0] = alpha_one
    coefficients_ref[1] = factor
    coefficients_ref[2] = alpha_two


def on_device(
    current_block, previous_block, beta_coupling, diagonal, blocks, near_index, far_index, counts
):
    tile_blocks = blocks[0, 0]
    lists = jnp.concatenate([near_index[0, 0], far_index[0, 0], counts[0]])
    nv, share = current_block.shape
    slots, width = tile_blocks.shape[:2]
    n_row, n_col = lax.axis_size("row"), lax.axis_size("col")
    rows_total = share * n_row * n_col
    products_scratch = pltpu.VMEM((slots, 2 * nv, width), F32)

    chunks = call(rounded_kernel, shape_of((n_col, 2 * nv, width), BF16), [VMEM])(current_block)
    constants = call(pack_kernel, shape_of((3 * nv, share)), [VMEM] * 4)(
        current_block, previous_block, beta_coupling, diagonal.reshape(1, share)
    )
    near_vectors = exchange(chunks, "col")
    far_vectors = exchange(chunks, "row")

    def products(over_columns, vectors, peers):
        return call(
            functools.partial(products_into, over_columns),
            shape_of((peers, 2, nv, width)),
            [SMEM, VMEM, VMEM],
            [products_scratch],
        )(lists, vectors, tile_blocks)

    far_got = exchange(products(False, near_vectors, n_row), "row")
    near_got = exchange(products(True, far_vectors, n_col), "col")
    state, chunks = call(
        middle_kernel,
        (shape_of((5 * nv, share)), shape_of((n_col, 2 * nv, width), BF16)),
        [VMEM] * 3,
    )(near_got, far_got, constants)

    near_vectors = exchange(chunks, "col")
    chunks, near_vectors = lax.optimization_barrier((chunks, near_vectors))
    far_vectors = exchange(chunks, "row")
    far_part = call(
        functools.partial(rounded_products_kernel, False),
        shape_of((n_row, 2 * nv, width), BF16),
        [SMEM, VMEM, VMEM],
        [products_scratch, pltpu.VMEM((n_row, 2, nv, width), F32)],
    )(lists, near_vectors, tile_blocks)
    near_part = call(
        near_kernel,
        shape_of((n_col, 2, 2 * nv, width), BF16),
        [SMEM] + [VMEM] * 4,
        [products_scratch, pltpu.VMEM((n_col, 2, nv, width), F32)],
    )(lists, far_vectors, near_vectors, tile_blocks, state)
    near_got = exchange(near_part, "col")
    near_sum, far_part = call(
        forward_kernel,
        (shape_of((2, nv, width)), shape_of((n_row, 2, 2 * nv, width), BF16)),
        [VMEM] * 2,
    )(near_got, far_part)
    far_got = exchange(far_part, "row")
    return call(
        functools.partial(last_kernel, rows_total),
        (shape_of((nv, share)), shape_of((nv, share)), shape_of((3, nv, nv))),
        [VMEM] * 3,
    )(near_sum, far_got, state)


def solution(mesh):
    return jax.shard_map(
        on_device,
        mesh=mesh,
        in_specs=(
            P(None, ("row", "col")),
            P(None, ("row", "col")),
            P(),
            P(("row", "col")),
            P("row", "col", None, None, None),
            P("row", "col", None),
            P("row", "col", None),
            P("row", "col"),
        ),
        out_specs=(P(None, ("row", "col")), P(None, ("row", "col")), P()),
        check_vma=False,
    )
```

```python
import functools

import jax
import jax.numpy as jnp
from jax import lax
from jax.experimental import pallas as pl
from jax.experimental.pallas import tpu as pltpu
from jax.sharding import PartitionSpec as P

HIGHEST = lax.Precision.HIGHEST
F32 = jnp.float32
BF16 = jnp.bfloat16
SHIFT = 1.25
VMEM = pl.BlockSpec(memory_space=pltpu.VMEM)
SMEM = pl.BlockSpec(memory_space=pltpu.SMEM)
PARAMS = pltpu.CompilerParams(vmem_limit_bytes=24 * 1024 * 1024)


def exchange(chunks, axis):
    return lax.all_to_all(chunks, axis, split_axis=0, concat_axis=0, tiled=True)


def call(kernel, out_shape, in_specs, scratch=()):
    many = isinstance(out_shape, (list, tuple))
    return pl.pallas_call(
        kernel,
        out_shape=out_shape,
        in_specs=in_specs,
        out_specs=tuple(VMEM for _ in out_shape) if many else VMEM,
        scratch_shapes=list(scratch),
        compiler_params=PARAMS,
    )


def shape_of(shape, dtype=F32):
    return jax.ShapeDtypeStruct(shape, dtype)


def pieces(ref):
    width = ref.shape[-1] // 2
    return [ref[:, :width], ref[:, width:]]


def contract_last(left, right):
    return lax.dot_general(
        left, right, (((1,), (1,)), ((), ())), precision=HIGHEST, preferred_element_type=F32
    )


def small_dot(left, right):
    total = left[:, 0:1] * right[0:1, :]
    for k in range(1, right.shape[0]):
        total = total + left[:, k : k + 1] * right[k : k + 1, :]
    return total


def identity(size):
    rows = lax.broadcasted_iota(jnp.int32, (size, size), 0)
    return (rows == lax.broadcasted_iota(jnp.int32, (size, size), 1)).astype(F32)


def split_two(values):
    high = values.astype(BF16)
    return high, (values - high.astype(F32)).astype(BF16)


def pack_extra(extra):
    high = extra.astype(BF16).astype(F32)
    rest = extra - high
    middle = rest.astype(BF16).astype(F32)
    low = rest - middle
    nv = extra.shape[0]
    return jnp.concatenate([high, middle, low[:, : 4 * nv]], axis=1)


def unpack_extra(total):
    nv = total.shape[0]
    low = jnp.concatenate([total[:, 12 * nv :], jnp.zeros((nv, 2 * nv), F32)], axis=1)
    return total[:, : 6 * nv] + (total[:, 6 * nv : 12 * nv] + low)


def rounded_kernel(vectors_ref, out_ref):
    chunk = jnp.concatenate(pieces(vectors_ref), axis=0).astype(BF16)
    out_ref[...] = jnp.broadcast_to(chunk[None], out_ref.shape)


def pack_kernel(current_ref, previous_ref, beta_ref, diagonal_ref, out_ref):
    nv = current_ref.shape[0]
    out_ref[:nv] = current_ref[...]
    out_ref[nv : 2 * nv] = small_dot(beta_ref[...], previous_ref[...])
    out_ref[2 * nv :] = jnp.broadcast_to(diagonal_ref[...], (nv, out_ref.shape[1]))


def products_kernel(over_columns, lists_ref, vectors_ref, blocks_ref, out_ref, products_ref):
    slots = blocks_ref.shape[0]
    src, dst = (slots, 0) if over_columns else (0, slots)
    nv = out_ref.shape[2]
    has_low = vectors_ref.shape[1] > 2 * nv
    dims = (((1,), (1 if over_columns else 0,)), ((), ()))
    for k in range(slots):
        pair = vectors_ref[lax.shift_right_logical(lists_ref[src + k], 1)]
        product = lax.dot_general(pair, blocks_ref[k], dims, preferred_element_type=F32)
        if has_low:
            product = product[: 2 * nv] + product[2 * nv :]
        products_ref[k] = product
    out_ref[...] = jnp.zeros_like(out_ref)

    def one_slot(k, carry):
        half = pl.multiple_of((lists_ref[src + k] & 1) * nv, nv)
        block = lists_ref[dst + k]
        out_ref[lax.shift_right_logical(block, 1), block & 1] += products_ref[
            k, pl.ds(half, nv), :
        ]
        return carry

    lax.fori_loop(0, lists_ref[2 * slots], one_slot, 0)


def quadratic_kernel(sums_ref, near_ref, state_ref, out_ref):
    nv, width = sums_ref.shape[2:]
    total = jnp.zeros((4 * nv, 4 * nv), F32)
    for n in range(out_ref.shape[0]):
        pair = jnp.concatenate([sums_ref[n, 0], sums_ref[n, 1]], axis=0)
        high, low = split_two(pair)
        total = total + lax.dot_general(
            jnp.concatenate([high, low], axis=0),
            near_ref[n],
            (((1,), (1,)), ((), ())),
            preferred_element_type=F32,
        )
    total = total[: 2 * nv] + total[2 * nv :]
    total = total[:, : 2 * nv] + total[:, 2 * nv :]
    quadratic = total[:nv, :nv] + total[nv:, nv:]
    quadratic = quadratic + contract_last(identity(nv), quadratic)
    shifted = state_ref[nv : 2 * nv]
    quadratic = quadratic + contract_last(shifted, state_ref[3 * nv : 4 * nv] * shifted)
    extra = pack_extra(jnp.concatenate([state_ref[4 * nv :, : 5 * nv], quadratic], axis=1))
    for n in range(out_ref.shape[0]):
        out_ref[n] = jnp.concatenate([sums_ref[n, 0], sums_ref[n, 1], extra], axis=0).astype(BF16)


def middle_kernel(near_ref, far_ref, constants_ref, state_ref, payload_ref):
    nv, width = near_ref.shape[2:]
    total = jnp.zeros((3 * nv, 3 * nv), F32)
    halves = []
    for t in range(2):
        part = slice(t * width, (t + 1) * width)
        current = constants_ref[:nv, part]
        diag = constants_ref[2 * nv :, part]
        off_diagonal = jnp.sum(near_ref[:, t], axis=0) + jnp.sum(far_ref[:, t], axis=0)
        applied = off_diagonal + diag * current
        shifted = applied - constants_ref[nv : 2 * nv, part] - SHIFT * current
        stack = jnp.concatenate([current, shifted, applied], axis=0)
        state_ref[: 3 * nv, part] = stack
        state_ref[3 * nv : 4 * nv, part] = diag
        total = total + contract_last(stack, stack)
        halves.append(shifted)
    pair = jnp.concatenate(halves, axis=0)
    high = pair.astype(BF16).astype(F32)
    chunk = jnp.concatenate([high, pair - high], axis=0).astype(BF16)
    payload_ref[...] = jnp.broadcast_to(chunk[None], payload_ref.shape)
    state_ref[4 * nv :] = jnp.concatenate(
        [
            total[:nv, :nv],
            total[nv : 2 * nv, nv : 2 * nv],
            total[:nv, nv : 2 * nv],
            total[nv : 2 * nv, 2 * nv :],
            total[:nv, 2 * nv :],
            jnp.zeros((nv, 2 * width - 5 * nv), F32),
        ],
        axis=1,
    )


def forward_kernel(near_ref, far_ref, state_ref, late_ref, out_ref):
    nv = far_ref.shape[2]
    width = far_ref.shape[3]
    total = jnp.sum(near_ref[...].astype(F32), axis=0)
    late_ref[: 3 * nv] = state_ref[: 3 * nv]
    for t in range(2):
        part = slice(t * width, (t + 1) * width)
        late_ref[3 * nv :, part] = (
            total[t * nv : (t + 1) * nv] + state_ref[3 * nv : 4 * nv, part] * state_ref[nv : 2 * nv, part]
        )
    extra = pack_extra(unpack_extra(total[2 * nv :]))
    for n in range(out_ref.shape[0]):
        out_ref[n] = jnp.concatenate([far_ref[n, 0], far_ref[n, 1], extra], axis=0).astype(BF16)


def last_kernel(rows_total, far_ref, state_ref, residual_ref, next_ref, coefficients_ref):
    nv, width = coefficients_ref.shape[1], far_ref.shape[2]
    received = jnp.sum(far_ref[...].astype(F32), axis=0)
    extra = unpack_extra(received[2 * nv :])
    gram = lambda i: extra[:, i * nv : (i + 1) * nv]
    cc, xx, cx, xu, cu, xw = (gram(i) for i in range(6))
    eye = identity(nv)
    xc = contract_last(eye, cx)
    scale = 1.0 / rows_total
    alpha_one = (cx + SHIFT * cc) * scale
    alpha = alpha_one - SHIFT * eye
    alpha_t = (xc + SHIFT * cc) * scale - SHIFT * eye
    adjusted_c = xc - small_dot(alpha_t, cc)
    work = (xx - small_dot(alpha_t, cx) - small_dot(adjusted_c, alpha)) * scale
    rows = lax.broadcasted_iota(jnp.int32, (nv, nv), 0)
    columns = lax.broadcasted_iota(jnp.int32, (nv, nv), 1)
    factor = jnp.zeros((nv, nv), F32)
    factor_t = jnp.zeros((nv, nv), F32)
    inverse = eye
    for j in range(nv):
        root = lax.rsqrt(work[j : j + 1, j : j + 1])
        column = jnp.where(rows[:, :1] >= j, work[:, j : j + 1] * root, 0.0)
        row = jnp.where(columns[:1] >= j, work[j : j + 1, :] * root, 0.0)
        factor = jnp.where(columns == j, column, factor)
        factor_t = jnp.where(rows == j, row, factor_t)
        work = work - column * row
        done = inverse[j : j + 1, :] * root
        below = jnp.where(rows[:, :1] > j, column, 0.0)
        inverse = jnp.where(rows == j, done, inverse - below * done)
    half = small_dot(xu, alpha)
    z = (
        xw
        - half
        - contract_last(eye, half)
        + small_dot(small_dot(alpha_t, cu), alpha)
    )
    alpha_two = contract_last(small_dot(inverse, z), inverse)
    alpha_two = (alpha_two - small_dot(small_dot(inverse, adjusted_c), factor)) * scale
    alpha_two_t = contract_last(eye, alpha_two)
    for t in range(2):
        part = slice(t * width, (t + 1) * width)
        current = state_ref[:nv, part]
        shifted = state_ref[nv : 2 * nv, part]
        applied = state_ref[2 * nv : 3 * nv, part]
        applied_shifted = state_ref[3 * nv :, part] + received[t * nv : (t + 1) * nv]
        following = small_dot(inverse, shifted - small_dot(alpha_t, current))
        second = small_dot(inverse, applied_shifted - small_dot(alpha_t, applied))
        second = second - small_dot(factor_t, current)
        next_ref[:, part] = following
        residual_ref[:, part] = second - small_dot(alpha_two_t, following)
    coefficients_ref[0] = alpha_one
    coefficients_ref[1] = factor
    coefficients_ref[2] = alpha_two


def on_device(
    current_block, previous_block, beta_coupling, diagonal, blocks, near_index, far_index, counts
):
    tile_blocks = blocks[0, 0]
    lists = jnp.concatenate([near_index[0, 0], far_index[0, 0], counts[0]])
    nv, share = current_block.shape
    slots, width = tile_blocks.shape[:2]
    n_row, n_col = lax.axis_size("row"), lax.axis_size("col")
    rows_total = share * n_row * n_col

    def products(over_columns, vectors, peers):
        return call(
            functools.partial(products_kernel, over_columns),
            shape_of((peers, 2, nv, width)),
            [SMEM, VMEM, VMEM],
            [pltpu.VMEM((slots, 2 * nv, width), F32)],
        )(lists, vectors, tile_blocks)

    chunks = call(rounded_kernel, shape_of((n_col, 2 * nv, width), BF16), [VMEM])(current_block)
    constants = call(pack_kernel, shape_of((3 * nv, share)), [VMEM] * 4)(
        current_block, previous_block, beta_coupling, diagonal.reshape(1, share)
    )
    lists, constants = lax.optimization_barrier((lists, constants))
    near_vectors = exchange(chunks, "col")
    far_vectors = exchange(chunks, "row")
    far_got = exchange(products(False, near_vectors, n_row), "row")
    near_got = exchange(products(True, far_vectors, n_col), "col")
    state, chunks = call(
        middle_kernel,
        (shape_of((5 * nv, share)), shape_of((n_col, 4 * nv, width), BF16)),
        [VMEM] * 3,
    )(near_got, far_got, constants)

    far_vectors = exchange(chunks, "row")
    chunks, far_vectors = lax.optimization_barrier((chunks, far_vectors))
    near_vectors = exchange(chunks, "col")
    near_part = products(True, far_vectors, n_col)
    near_part = call(quadratic_kernel, shape_of((n_col, 3 * nv, width), BF16), [VMEM] * 3)(
        near_part, near_vectors, state
    )
    near_got = exchange(near_part, "col")
    far_part = products(False, near_vectors, n_row)
    late, far_part = call(
        forward_kernel,
        (shape_of((4 * nv, share)), shape_of((n_row, 3 * nv, width), BF16)),
        [VMEM] * 3,
    )(near_got, far_part, state)
    far_got = exchange(far_part, "row")
    return call(
        functools.partial(last_kernel, rows_total),
        (shape_of((nv, share)), shape_of((nv, share)), shape_of((3, nv, nv))),
        [VMEM] * 2,
    )(far_got, late)


def solution(mesh):
    return jax.shard_map(
        on_device,
        mesh=mesh,
        in_specs=(
            P(None, ("row", "col")),
            P(None, ("row", "col")),
            P(),
            P(("row", "col")),
            P("row", "col", None, None, None),
            P("row", "col", None),
            P("row", "col", None),
            P("row", "col"),
        ),
        out_specs=(P(None, ("row", "col")), P(None, ("row", "col")), P()),
        check_vma=False,
    )
```

```python
import functools

import jax
import jax.numpy as jnp
from jax import lax
from jax.experimental import pallas as pl
from jax.experimental.pallas import tpu as pltpu
from jax.sharding import PartitionSpec as P

HIGHEST = lax.Precision.HIGHEST
F32 = jnp.float32
BF16 = jnp.bfloat16
SHIFT = 1.25
VMEM = pl.BlockSpec(memory_space=pltpu.VMEM)
SMEM = pl.BlockSpec(memory_space=pltpu.SMEM)
PARAMS = pltpu.CompilerParams(vmem_limit_bytes=24 * 1024 * 1024)


def exchange(chunks, axis):
    return lax.all_to_all(chunks, axis, split_axis=0, concat_axis=0, tiled=True)


def call(kernel, out_shape, in_specs, scratch=()):
    many = isinstance(out_shape, (list, tuple))
    return pl.pallas_call(
        kernel,
        out_shape=out_shape,
        in_specs=in_specs,
        out_specs=tuple(VMEM for _ in out_shape) if many else VMEM,
        scratch_shapes=list(scratch),
        compiler_params=PARAMS,
    )


def shape_of(shape, dtype=F32):
    return jax.ShapeDtypeStruct(shape, dtype)


def pieces(ref):
    width = ref.shape[-1] // 2
    return [ref[:, :width], ref[:, width:]]


def contract_last(left, right):
    return lax.dot_general(
        left, right, (((1,), (1,)), ((), ())), precision=HIGHEST, preferred_element_type=F32
    )


def small_dot(left, right):
    total = left[:, 0:1] * right[0:1, :]
    for k in range(1, right.shape[0]):
        total = total + left[:, k : k + 1] * right[k : k + 1, :]
    return total


def identity(size):
    rows = lax.broadcasted_iota(jnp.int32, (size, size), 0)
    return (rows == lax.broadcasted_iota(jnp.int32, (size, size), 1)).astype(F32)


def split_two(values):
    high = values.astype(BF16)
    return high, (values - high.astype(F32)).astype(BF16)


def pack_extra(extra):
    high = extra.astype(BF16).astype(F32)
    rest = extra - high
    middle = rest.astype(BF16).astype(F32)
    low = rest - middle
    nv = extra.shape[0]
    return jnp.concatenate([high, middle, low[:, : 4 * nv]], axis=1)


def unpack_extra(total):
    nv = total.shape[0]
    low = jnp.concatenate([total[:, 12 * nv :], jnp.zeros((nv, 2 * nv), F32)], axis=1)
    return total[:, : 6 * nv] + (total[:, 6 * nv : 12 * nv] + low)


def rounded_kernel(vectors_ref, out_ref):
    chunk = jnp.concatenate(pieces(vectors_ref), axis=0).astype(BF16)
    out_ref[...] = jnp.broadcast_to(chunk[None], out_ref.shape)


def pack_kernel(
    current_ref, previous_ref, beta_ref, diagonal_ref, blocks_ref, out_ref, held_ref
):
    nv = current_ref.shape[0]
    held_ref[...] = blocks_ref[...]
    out_ref[:nv] = current_ref[...]
    out_ref[nv : 2 * nv] = small_dot(beta_ref[...], previous_ref[...])
    out_ref[2 * nv :] = jnp.broadcast_to(diagonal_ref[...], (nv, out_ref.shape[1]))


def place_products(
    lists_ref, near_ref, far_ref, blocks_ref, near_out, far_out, near_products, far_products
):
    slots = blocks_ref.shape[0]
    nv = near_out.shape[2]

    def product(ref, index, block, block_dim):
        pair = ref[lax.shift_right_logical(index, 1)]
        values = lax.dot_general(
            pair, block, (((1,), (block_dim,)), ((), ())), preferred_element_type=F32
        )
        if ref.shape[1] > 2 * nv:
            values = values[: 2 * nv] + values[2 * nv :]
        return values

    for k in range(slots):
        block = blocks_ref[k]
        near_products[k] = product(far_ref, lists_ref[slots + k], block, 1)
        far_products[k] = product(near_ref, lists_ref[k], block, 0)
    near_out[...] = jnp.zeros_like(near_out)
    far_out[...] = jnp.zeros_like(far_out)

    def one_slot(k, carry):
        near, far = lists_ref[k], lists_ref[slots + k]
        near_half, far_half = near & 1, far & 1
        near_chunk, far_chunk = lax.shift_right_logical(near, 1), lax.shift_right_logical(far, 1)
        near_out[near_chunk, near_half] += near_products[
            k, pl.ds(pl.multiple_of(far_half * nv, nv), nv), :
        ]
        far_out[far_chunk, far_half] += far_products[
            k, pl.ds(pl.multiple_of(near_half * nv, nv), nv), :
        ]
        return carry

    lax.fori_loop(0, lists_ref[2 * slots], one_slot, 0)


def second_kernel(
    lists_ref,
    near_ref,
    far_ref,
    blocks_ref,
    state_ref,
    out_ref,
    far_out,
    near_products,
    far_products,
    sums_ref,
):
    place_products(
        lists_ref, near_ref, far_ref, blocks_ref, sums_ref, far_out, near_products, far_products
    )
    nv, width = sums_ref.shape[2:]
    total = jnp.zeros((4 * nv, 4 * nv), F32)
    for n in range(out_ref.shape[0]):
        pair = jnp.concatenate([sums_ref[n, 0], sums_ref[n, 1]], axis=0)
        high, low = split_two(pair)
        total = total + lax.dot_general(
            jnp.concatenate([high, low], axis=0),
            near_ref[n],
            (((1,), (1,)), ((), ())),
            preferred_element_type=F32,
        )
    total = total[: 2 * nv] + total[2 * nv :]
    total = total[:, : 2 * nv] + total[:, 2 * nv :]
    quadratic = total[:nv, :nv] + total[nv:, nv:]
    quadratic = quadratic + contract_last(identity(nv), quadratic)
    shifted = state_ref[nv : 2 * nv]
    quadratic = quadratic + contract_last(shifted, state_ref[3 * nv : 4 * nv] * shifted)
    extra = pack_extra(jnp.concatenate([state_ref[4 * nv :, : 5 * nv], quadratic], axis=1))
    for n in range(out_ref.shape[0]):
        out_ref[n] = jnp.concatenate([sums_ref[n, 0], sums_ref[n, 1], extra], axis=0).astype(BF16)


def middle_kernel(near_ref, far_ref, constants_ref, state_ref, payload_ref):
    nv, width = near_ref.shape[2:]
    total = jnp.zeros((3 * nv, 3 * nv), F32)
    halves = []
    for t in range(2):
        part = slice(t * width, (t + 1) * width)
        current = constants_ref[:nv, part]
        diag = constants_ref[2 * nv :, part]
        off_diagonal = jnp.sum(near_ref[:, t], axis=0) + jnp.sum(far_ref[:, t], axis=0)
        applied = off_diagonal + diag * current
        shifted = applied - constants_ref[nv : 2 * nv, part] - SHIFT * current
        stack = jnp.concatenate([current, shifted, applied], axis=0)
        state_ref[: 3 * nv, part] = stack
        state_ref[3 * nv : 4 * nv, part] = diag
        total = total + contract_last(stack, stack)
        halves.append(shifted)
    pair = jnp.concatenate(halves, axis=0)
    high = pair.astype(BF16).astype(F32)
    chunk = jnp.concatenate([high, pair - high], axis=0).astype(BF16)
    payload_ref[...] = jnp.broadcast_to(chunk[None], payload_ref.shape)
    state_ref[4 * nv :] = jnp.concatenate(
        [
            total[:nv, :nv],
            total[nv : 2 * nv, nv : 2 * nv],
            total[:nv, nv : 2 * nv],
            total[nv : 2 * nv, 2 * nv :],
            total[:nv, 2 * nv :],
            jnp.zeros((nv, 2 * width - 5 * nv), F32),
        ],
        axis=1,
    )


def forward_kernel(near_ref, far_ref, state_ref, late_ref, out_ref):
    nv = far_ref.shape[2]
    width = far_ref.shape[3]
    total = jnp.sum(near_ref[...].astype(F32), axis=0)
    late_ref[: 3 * nv] = state_ref[: 3 * nv]
    for t in range(2):
        part = slice(t * width, (t + 1) * width)
        late_ref[3 * nv :, part] = (
            total[t * nv : (t + 1) * nv] + state_ref[3 * nv : 4 * nv, part] * state_ref[nv : 2 * nv, part]
        )
    extra = pack_extra(unpack_extra(total[2 * nv :]))
    for n in range(out_ref.shape[0]):
        out_ref[n] = jnp.concatenate([far_ref[n, 0], far_ref[n, 1], extra], axis=0).astype(BF16)


def last_kernel(rows_total, far_ref, state_ref, residual_ref, next_ref, coefficients_ref):
    nv, width = coefficients_ref.shape[1], far_ref.shape[2]
    received = jnp.sum(far_ref[...].astype(F32), axis=0)
    extra = unpack_extra(received[2 * nv :])
    gram = lambda i: extra[:, i * nv : (i + 1) * nv]
    cc, xx, cx, xu, cu, xw = (gram(i) for i in range(6))
    eye = identity(nv)
    xc = contract_last(eye, cx)
    scale = 1.0 / rows_total
    alpha_one = (cx + SHIFT * cc) * scale
    alpha = alpha_one - SHIFT * eye
    alpha_t = (xc + SHIFT * cc) * scale - SHIFT * eye
    adjusted_c = xc - small_dot(alpha_t, cc)
    work = (xx - small_dot(alpha_t, cx) - small_dot(adjusted_c, alpha)) * scale
    rows = lax.broadcasted_iota(jnp.int32, (nv, nv), 0)
    columns = lax.broadcasted_iota(jnp.int32, (nv, nv), 1)
    factor = jnp.zeros((nv, nv), F32)
    factor_t = jnp.zeros((nv, nv), F32)
    inverse = eye
    for j in range(nv):
        root = lax.rsqrt(work[j : j + 1, j : j + 1])
        column = jnp.where(rows[:, :1] >= j, work[:, j : j + 1] * root, 0.0)
        row = jnp.where(columns[:1] >= j, work[j : j + 1, :] * root, 0.0)
        factor = jnp.where(columns == j, column, factor)
        factor_t = jnp.where(rows == j, row, factor_t)
        work = work - column * row
        done = inverse[j : j + 1, :] * root
        below = jnp.where(rows[:, :1] > j, column, 0.0)
        inverse = jnp.where(rows == j, done, inverse - below * done)
    half = small_dot(xu, alpha)
    z = (
        xw
        - half
        - contract_last(eye, half)
        + small_dot(small_dot(alpha_t, cu), alpha)
    )
    alpha_two = contract_last(small_dot(inverse, z), inverse)
    alpha_two = (alpha_two - small_dot(small_dot(inverse, adjusted_c), factor)) * scale
    alpha_two_t = contract_last(eye, alpha_two)
    for t in range(2):
        part = slice(t * width, (t + 1) * width)
        current = state_ref[:nv, part]
        shifted = state_ref[nv : 2 * nv, part]
        applied = state_ref[2 * nv : 3 * nv, part]
        applied_shifted = state_ref[3 * nv :, part] + received[t * nv : (t + 1) * nv]
        following = small_dot(inverse, shifted - small_dot(alpha_t, current))
        second = small_dot(inverse, applied_shifted - small_dot(alpha_t, applied))
        second = second - small_dot(factor_t, current)
        next_ref[:, part] = following
        residual_ref[:, part] = second - small_dot(alpha_two_t, following)
    coefficients_ref[0] = alpha_one
    coefficients_ref[1] = factor
    coefficients_ref[2] = alpha_two


def on_device(
    current_block, previous_block, beta_coupling, diagonal, blocks, near_index, far_index, counts
):
    tile_blocks = blocks[0, 0]
    lists = jnp.concatenate([near_index[0, 0], far_index[0, 0], counts[0]])
    nv, share = current_block.shape
    slots, width = tile_blocks.shape[:2]
    n_row, n_col = lax.axis_size("row"), lax.axis_size("col")
    rows_total = share * n_row * n_col
    near_sums, far_sums = (n_col, 2, nv, width), (n_row, 2, nv, width)
    products_scratch = [pltpu.VMEM((slots, 2 * nv, width), F32)] * 2

    chunks = call(rounded_kernel, shape_of((n_col, 2 * nv, width), BF16), [VMEM])(current_block)
    constants, held_blocks = call(
        pack_kernel, (shape_of((3 * nv, share)), shape_of(tile_blocks.shape, BF16)), [VMEM] * 5
    )(current_block, previous_block, beta_coupling, diagonal.reshape(1, share), tile_blocks)
    near_vectors = exchange(chunks, "col")
    far_vectors = exchange(chunks, "row")
    near_part, far_part = call(
        place_products,
        (shape_of(near_sums), shape_of(far_sums)),
        [SMEM, VMEM, VMEM, VMEM],
        products_scratch,
    )(lists, near_vectors, far_vectors, held_blocks)
    far_got = exchange(far_part, "row")
    near_got = exchange(near_part, "col")
    state, chunks = call(
        middle_kernel,
        (shape_of((5 * nv, share)), shape_of((n_col, 4 * nv, width), BF16)),
        [VMEM] * 3,
    )(near_got, far_got, constants)

    far_vectors = exchange(chunks, "row")
    near_vectors = exchange(chunks, "col")
    near_part, far_part = call(
        second_kernel,
        (shape_of((n_col, 3 * nv, width), BF16), shape_of(far_sums)),
        [SMEM, VMEM, VMEM, VMEM, VMEM],
        products_scratch + [pltpu.VMEM(near_sums, F32)],
    )(lists, near_vectors, far_vectors, held_blocks, state)
    near_got = exchange(near_part, "col")
    late, far_part = call(
        forward_kernel,
        (shape_of((4 * nv, share)), shape_of((n_row, 3 * nv, width), BF16)),
        [VMEM] * 3,
    )(near_got, far_part, state)
    far_got = exchange(far_part, "row")
    return call(
        functools.partial(last_kernel, rows_total),
        (shape_of((nv, share)), shape_of((nv, share)), shape_of((3, nv, nv))),
        [VMEM] * 2,
    )(far_got, late)


def solution(mesh):
    return jax.shard_map(
        on_device,
        mesh=mesh,
        in_specs=(
            P(None, ("row", "col")),
            P(None, ("row", "col")),
            P(),
            P(("row", "col")),
            P("row", "col", None, None, None),
            P("row", "col", None),
            P("row", "col", None),
            P("row", "col"),
        ),
        out_specs=(P(None, ("row", "col")), P(None, ("row", "col")), P()),
        check_vma=False,
    )
```

```python
import functools

import jax
import jax.numpy as jnp
from jax import lax
from jax.experimental import pallas as pl
from jax.experimental.pallas import tpu as pltpu
from jax.sharding import PartitionSpec as P

HIGHEST = lax.Precision.HIGHEST
F32 = jnp.float32
BF16 = jnp.bfloat16
SHIFT = 1.25
VMEM = pl.BlockSpec(memory_space=pltpu.VMEM)
SMEM = pl.BlockSpec(memory_space=pltpu.SMEM)
PARAMS = pltpu.CompilerParams(vmem_limit_bytes=24 * 1024 * 1024)


def exchange(chunks, axis):
    return lax.all_to_all(chunks, axis, split_axis=0, concat_axis=0, tiled=True)


def call(kernel, out_shape, in_specs, scratch=()):
    many = isinstance(out_shape, (list, tuple))
    return pl.pallas_call(
        kernel,
        out_shape=out_shape,
        in_specs=in_specs,
        out_specs=tuple(VMEM for _ in out_shape) if many else VMEM,
        scratch_shapes=list(scratch),
        compiler_params=PARAMS,
    )


def shape_of(shape, dtype=F32):
    return jax.ShapeDtypeStruct(shape, dtype)


def pieces(ref):
    width = ref.shape[-1] // 2
    return [ref[:, :width], ref[:, width:]]


def contract_last(left, right):
    return lax.dot_general(
        left, right, (((1,), (1,)), ((), ())), precision=HIGHEST, preferred_element_type=F32
    )


def small_dot(left, right):
    total = left[:, 0:1] * right[0:1, :]
    for k in range(1, right.shape[0]):
        total = total + left[:, k : k + 1] * right[k : k + 1, :]
    return total


def transposed(matrix):
    size = matrix.shape[0]
    tile = jnp.concatenate([matrix, jnp.zeros((size, 128 - size), F32)], axis=1)
    return jnp.transpose(tile)[:size]


def identity(size):
    rows = lax.broadcasted_iota(jnp.int32, (size, size), 0)
    return (rows == lax.broadcasted_iota(jnp.int32, (size, size), 1)).astype(F32)


def split_two(values):
    high = values.astype(BF16)
    return high, (values - high.astype(F32)).astype(BF16)


def pack_extra(extra):
    high = extra.astype(BF16).astype(F32)
    rest = extra - high
    middle = rest.astype(BF16).astype(F32)
    low = rest - middle
    nv = extra.shape[0]
    return jnp.concatenate([high, middle, low[:, : 4 * nv]], axis=1)


def unpack_extra(total):
    nv = total.shape[0]
    low = jnp.concatenate([total[:, 12 * nv :], jnp.zeros((nv, 2 * nv), F32)], axis=1)
    return total[:, : 6 * nv] + (total[:, 6 * nv : 12 * nv] + low)


def rounded_kernel(vectors_ref, out_ref):
    chunk = jnp.concatenate(pieces(vectors_ref), axis=0).astype(BF16)
    out_ref[...] = jnp.broadcast_to(chunk[None], out_ref.shape)


def pack_kernel(
    current_ref, previous_ref, beta_ref, diagonal_ref, blocks_ref, out_ref, held_ref
):
    nv = current_ref.shape[0]
    held_ref[...] = blocks_ref[...]
    out_ref[:nv] = current_ref[...]
    out_ref[nv : 2 * nv] = small_dot(beta_ref[...], previous_ref[...])
    out_ref[2 * nv :] = jnp.broadcast_to(diagonal_ref[...], (nv, out_ref.shape[1]))


def place_products(
    lists_ref, near_ref, far_ref, blocks_ref, near_out, far_out, near_products, far_products
):
    slots = blocks_ref.shape[0]
    nv = near_out.shape[2]

    def product(ref, index, block, block_dim):
        pair = ref[lax.shift_right_logical(index, 1)]
        values = lax.dot_general(
            pair, block, (((1,), (block_dim,)), ((), ())), preferred_element_type=F32
        )
        if ref.shape[1] > 2 * nv:
            values = values[: 2 * nv] + values[2 * nv :]
        return values

    for k in range(slots):
        block = blocks_ref[k]
        near_products[k] = product(far_ref, lists_ref[slots + k], block, 1)
        far_products[k] = product(near_ref, lists_ref[k], block, 0)
    near_out[...] = jnp.zeros_like(near_out)
    far_out[...] = jnp.zeros_like(far_out)

    def one_slot(k, carry):
        near, far = lists_ref[k], lists_ref[slots + k]
        near_half, far_half = near & 1, far & 1
        near_chunk, far_chunk = lax.shift_right_logical(near, 1), lax.shift_right_logical(far, 1)
        near_out[near_chunk, near_half] += near_products[
            k, pl.ds(pl.multiple_of(far_half * nv, nv), nv), :
        ]
        far_out[far_chunk, far_half] += far_products[
            k, pl.ds(pl.multiple_of(near_half * nv, nv), nv), :
        ]
        return carry

    lax.fori_loop(0, lists_ref[2 * slots], one_slot, 0)


def first_kernel(
    lists_ref,
    near_ref,
    far_ref,
    blocks_ref,
    near_out,
    far_out,
    near_products,
    far_products,
    near_sums,
    far_sums,
):
    place_products(
        lists_ref, near_ref, far_ref, blocks_ref, near_sums, far_sums, near_products, far_products
    )
    for out_ref, sums_ref in ((near_out, near_sums), (far_out, far_sums)):
        for n in range(out_ref.shape[0]):
            out_ref[n] = jnp.concatenate([sums_ref[n, 0], sums_ref[n, 1]], axis=0).astype(BF16)


def second_kernel(
    lists_ref,
    near_ref,
    far_ref,
    blocks_ref,
    state_ref,
    out_ref,
    far_out,
    near_products,
    far_products,
    sums_ref,
):
    place_products(
        lists_ref, near_ref, far_ref, blocks_ref, sums_ref, far_out, near_products, far_products
    )
    nv, width = sums_ref.shape[2:]
    total = jnp.zeros((4 * nv, 4 * nv), F32)
    for n in range(out_ref.shape[0]):
        pair = jnp.concatenate([sums_ref[n, 0], sums_ref[n, 1]], axis=0)
        high, low = split_two(pair)
        total = total + lax.dot_general(
            jnp.concatenate([high, low], axis=0),
            near_ref[n],
            (((1,), (1,)), ((), ())),
            preferred_element_type=F32,
        )
    total = total[: 2 * nv] + total[2 * nv :]
    total = total[:, : 2 * nv] + total[:, 2 * nv :]
    quadratic = total[:nv, :nv] + total[nv:, nv:]
    quadratic = quadratic + contract_last(identity(nv), quadratic)
    shifted = state_ref[nv : 2 * nv]
    quadratic = quadratic + contract_last(shifted, state_ref[3 * nv : 4 * nv] * shifted)
    extra = pack_extra(jnp.concatenate([state_ref[4 * nv :, : 5 * nv], quadratic], axis=1))
    for n in range(out_ref.shape[0]):
        out_ref[n] = jnp.concatenate([sums_ref[n, 0], sums_ref[n, 1], extra], axis=0).astype(BF16)


def middle_kernel(near_ref, far_ref, constants_ref, state_ref, payload_ref):
    nv, width = near_ref.shape[1] // 2, near_ref.shape[2]
    off = jnp.sum(near_ref[...].astype(F32), axis=0) + jnp.sum(far_ref[...].astype(F32), axis=0)
    total = jnp.zeros((3 * nv, 3 * nv), F32)
    halves = []
    for t in range(2):
        part = slice(t * width, (t + 1) * width)
        current = constants_ref[:nv, part]
        diag = constants_ref[2 * nv :, part]
        applied = off[t * nv : (t + 1) * nv] + diag * current
        shifted = applied - constants_ref[nv : 2 * nv, part] - SHIFT * current
        stack = jnp.concatenate([current, shifted, applied], axis=0)
        state_ref[: 3 * nv, part] = stack
        state_ref[3 * nv : 4 * nv, part] = diag
        total = total + contract_last(stack, stack)
        halves.append(shifted)
    pair = jnp.concatenate(halves, axis=0)
    high = pair.astype(BF16).astype(F32)
    chunk = jnp.concatenate([high, pair - high], axis=0).astype(BF16)
    payload_ref[...] = jnp.broadcast_to(chunk[None], payload_ref.shape)
    state_ref[4 * nv :] = jnp.concatenate(
        [
            total[:nv, :nv],
            total[nv : 2 * nv, nv : 2 * nv],
            total[:nv, nv : 2 * nv],
            total[nv : 2 * nv, 2 * nv :],
            total[:nv, 2 * nv :],
            jnp.zeros((nv, 2 * width - 5 * nv), F32),
        ],
        axis=1,
    )


def forward_kernel(near_ref, far_ref, state_ref, late_ref, out_ref):
    nv = far_ref.shape[2]
    width = far_ref.shape[3]
    total = jnp.sum(near_ref[...].astype(F32), axis=0)
    late_ref[: 3 * nv] = state_ref[: 3 * nv]
    for t in range(2):
        part = slice(t * width, (t + 1) * width)
        late_ref[3 * nv :, part] = (
            total[t * nv : (t + 1) * nv] + state_ref[3 * nv : 4 * nv, part] * state_ref[nv : 2 * nv, part]
        )
    extra = pack_extra(unpack_extra(total[2 * nv :]))
    for n in range(out_ref.shape[0]):
        out_ref[n] = jnp.concatenate([far_ref[n, 0], far_ref[n, 1], extra], axis=0).astype(BF16)


def last_kernel(rows_total, far_ref, state_ref, residual_ref, next_ref, coefficients_ref):
    nv, width = coefficients_ref.shape[1], far_ref.shape[2]
    received = jnp.sum(far_ref[...].astype(F32), axis=0)
    extra = unpack_extra(received[2 * nv :])
    gram = lambda i: extra[:, i * nv : (i + 1) * nv]
    cc, xx, cx, xu, cu, xw = (gram(i) for i in range(6))
    eye = identity(nv)
    xc = transposed(cx)
    scale = 1.0 / rows_total
    alpha_one = (cx + SHIFT * cc) * scale
    alpha = alpha_one - SHIFT * eye
    alpha_t = (xc + SHIFT * cc) * scale - SHIFT * eye
    adjusted_c = xc - small_dot(alpha_t, cc)
    work = (xx - small_dot(alpha_t, cx) - small_dot(adjusted_c, alpha)) * scale
    rows = lax.broadcasted_iota(jnp.int32, (nv, nv), 0)
    columns = lax.broadcasted_iota(jnp.int32, (nv, nv), 1)
    factor = jnp.zeros((nv, nv), F32)
    factor_t = jnp.zeros((nv, nv), F32)
    inverse = eye
    inverse_t = eye
    for j in range(nv):
        root = lax.rsqrt(work[j : j + 1, j : j + 1])
        column = jnp.where(rows[:, :1] >= j, work[:, j : j + 1] * root, 0.0)
        row = jnp.where(columns[:1] >= j, work[j : j + 1, :] * root, 0.0)
        factor = jnp.where(columns == j, column, factor)
        factor_t = jnp.where(rows == j, row, factor_t)
        work = work - column * row
        done = inverse[j : j + 1, :] * root
        below = jnp.where(rows[:, :1] > j, column, 0.0)
        inverse = jnp.where(rows == j, done, inverse - below * done)
        done_t = inverse_t[:, j : j + 1] * root
        right = jnp.where(columns[:1] > j, row, 0.0)
        inverse_t = jnp.where(columns == j, done_t, inverse_t - done_t * right)
    half = small_dot(xu, alpha)
    z = (
        xw
        - half
        - transposed(half)
        + small_dot(small_dot(alpha_t, cu), alpha)
    )
    alpha_two = small_dot(small_dot(inverse, z), inverse_t)
    alpha_two = (alpha_two - small_dot(small_dot(inverse, adjusted_c), factor)) * scale
    alpha_two_t = transposed(alpha_two)
    for t in range(2):
        part = slice(t * width, (t + 1) * width)
        current = state_ref[:nv, part]
        shifted = state_ref[nv : 2 * nv, part]
        applied = state_ref[2 * nv : 3 * nv, part]
        applied_shifted = state_ref[3 * nv :, part] + received[t * nv : (t + 1) * nv]
        following = small_dot(inverse, shifted - small_dot(alpha_t, current))
        second = small_dot(inverse, applied_shifted - small_dot(alpha_t, applied))
        second = second - small_dot(factor_t, current)
        next_ref[:, part] = following
        residual_ref[:, part] = second - small_dot(alpha_two_t, following)
    coefficients_ref[0] = alpha_one
    coefficients_ref[1] = factor
    coefficients_ref[2] = alpha_two


def on_device(
    current_block, previous_block, beta_coupling, diagonal, blocks, near_index, far_index, counts
):
    tile_blocks = blocks[0, 0]
    lists = jnp.concatenate([near_index[0, 0], far_index[0, 0], counts[0]])
    nv, share = current_block.shape
    slots, width = tile_blocks.shape[:2]
    n_row, n_col = lax.axis_size("row"), lax.axis_size("col")
    rows_total = share * n_row * n_col
    near_sums, far_sums = (n_col, 2, nv, width), (n_row, 2, nv, width)
    products_scratch = [pltpu.VMEM((slots, 2 * nv, width), F32)] * 2

    chunks = call(rounded_kernel, shape_of((n_col, 2 * nv, width), BF16), [VMEM])(current_block)
    constants, held_blocks = call(
        pack_kernel, (shape_of((3 * nv, share)), shape_of(tile_blocks.shape, BF16)), [VMEM] * 5
    )(current_block, previous_block, beta_coupling, diagonal.reshape(1, share), tile_blocks)
    near_vectors = exchange(chunks, "col")
    far_vectors = exchange(chunks, "row")
    near_part, far_part = call(
        first_kernel,
        (shape_of((n_col, 2 * nv, width), BF16), shape_of((n_row, 2 * nv, width), BF16)),
        [SMEM, VMEM, VMEM, VMEM],
        products_scratch + [pltpu.VMEM(near_sums, F32), pltpu.VMEM(far_sums, F32)],
    )(lists, near_vectors, far_vectors, held_blocks)
    far_got = exchange(far_part, "row")
    near_got = exchange(near_part, "col")
    state, chunks = call(
        middle_kernel,
        (shape_of((5 * nv, share)), shape_of((n_col, 4 * nv, width), BF16)),
        [VMEM] * 3,
    )(near_got, far_got, constants)

    far_vectors = exchange(chunks, "row")
    near_vectors = exchange(chunks, "col")
    near_part, far_part = call(
        second_kernel,
        (shape_of((n_col, 3 * nv, width), BF16), shape_of(far_sums)),
        [SMEM, VMEM, VMEM, VMEM, VMEM],
        products_scratch + [pltpu.VMEM(near_sums, F32)],
    )(lists, near_vectors, far_vectors, held_blocks, state)
    near_got = exchange(near_part, "col")
    late, far_part = call(
        forward_kernel,
        (shape_of((4 * nv, share)), shape_of((n_row, 3 * nv, width), BF16)),
        [VMEM] * 3,
    )(near_got, far_part, state)
    far_got = exchange(far_part, "row")
    return call(
        functools.partial(last_kernel, rows_total),
        (shape_of((nv, share)), shape_of((nv, share)), shape_of((3, nv, nv))),
        [VMEM] * 2,
    )(far_got, late)


def solution(mesh):
    return jax.shard_map(
        on_device,
        mesh=mesh,
        in_specs=(
            P(None, ("row", "col")),
            P(None, ("row", "col")),
            P(),
            P(("row", "col")),
            P("row", "col", None, None, None),
            P("row", "col", None),
            P("row", "col", None),
            P("row", "col"),
        ),
        out_specs=(P(None, ("row", "col")), P(None, ("row", "col")), P()),
        check_vma=False,
    )
```

```python
import functools

import jax
import jax.numpy as jnp
from jax import lax
from jax.experimental import pallas as pl
from jax.experimental.pallas import tpu as pltpu
from jax.sharding import PartitionSpec as P

HIGHEST = lax.Precision.HIGHEST
F32 = jnp.float32
BF16 = jnp.bfloat16
SHIFT = 1.25
VMEM = pl.BlockSpec(memory_space=pltpu.VMEM)
SMEM = pl.BlockSpec(memory_space=pltpu.SMEM)
PARAMS = pltpu.CompilerParams(vmem_limit_bytes=24 * 1024 * 1024)


def exchange(chunks, axis):
    return lax.all_to_all(chunks, axis, split_axis=0, concat_axis=0, tiled=True)


def call(kernel, out_shape, in_specs, scratch=()):
    many = isinstance(out_shape, (list, tuple))
    return pl.pallas_call(
        kernel,
        out_shape=out_shape,
        in_specs=in_specs,
        out_specs=tuple(VMEM for _ in out_shape) if many else VMEM,
        scratch_shapes=list(scratch),
        compiler_params=PARAMS,
    )


def shape_of(shape, dtype=F32):
    return jax.ShapeDtypeStruct(shape, dtype)


def pieces(ref):
    width = ref.shape[-1] // 2
    return [ref[:, :width], ref[:, width:]]


def contract_last(left, right):
    return lax.dot_general(
        left, right, (((1,), (1,)), ((), ())), precision=HIGHEST, preferred_element_type=F32
    )


def small_dot(left, right):
    total = left[:, 0:1] * right[0:1, :]
    for k in range(1, right.shape[0]):
        total = total + left[:, k : k + 1] * right[k : k + 1, :]
    return total


def transposed(matrix):
    size = matrix.shape[0]
    tile = jnp.concatenate([matrix, jnp.zeros((size, 128 - size), F32)], axis=1)
    return jnp.transpose(tile)[:size]


def identity(size):
    rows = lax.broadcasted_iota(jnp.int32, (size, size), 0)
    return (rows == lax.broadcasted_iota(jnp.int32, (size, size), 1)).astype(F32)


def split_two(values):
    high = values.astype(BF16)
    return high, (values - high.astype(F32)).astype(BF16)


def pack_extra(extra):
    high = extra.astype(BF16).astype(F32)
    rest = extra - high
    middle = rest.astype(BF16).astype(F32)
    low = rest - middle
    nv = extra.shape[0]
    return jnp.concatenate([high, middle, low[:, : 4 * nv]], axis=1)


def unpack_extra(total):
    nv = total.shape[0]
    low = jnp.concatenate([total[:, 12 * nv :], jnp.zeros((nv, 2 * nv), F32)], axis=1)
    return total[:, : 6 * nv] + (total[:, 6 * nv : 12 * nv] + low)


def rounded_kernel(vectors_ref, out_ref):
    chunk = jnp.concatenate(pieces(vectors_ref), axis=0).astype(BF16)
    out_ref[...] = jnp.broadcast_to(chunk[None], out_ref.shape)


def pack_kernel(
    current_ref, previous_ref, beta_ref, diagonal_ref, blocks_ref, out_ref, held_ref
):
    nv = current_ref.shape[0]
    held_ref[...] = blocks_ref[...]
    out_ref[:nv] = current_ref[...]
    out_ref[nv : 2 * nv] = small_dot(beta_ref[...], previous_ref[...])
    out_ref[2 * nv :] = jnp.broadcast_to(diagonal_ref[...], (nv, out_ref.shape[1]))


def place_products(lists_ref, near_ref, far_ref, blocks_ref, near_out, far_out):
    slots = blocks_ref.shape[0]
    nv = near_out.shape[2]

    def product(ref, index, block, block_dim):
        pair = ref[lax.shift_right_logical(index, 1)]
        values = lax.dot_general(
            pair, block, (((1,), (block_dim,)), ((), ())), preferred_element_type=F32
        )
        if ref.shape[1] > 2 * nv:
            values = values[: 2 * nv] + values[2 * nv :]
        return values

    near_out[...] = jnp.zeros_like(near_out)
    far_out[...] = jnp.zeros_like(far_out)
    live = lists_ref[2 * slots]
    for k in range(slots):
        near, far = lists_ref[k], lists_ref[slots + k]
        near_half, far_half = near & 1, far & 1
        near_chunk, far_chunk = lax.shift_right_logical(near, 1), lax.shift_right_logical(far, 1)
        block = blocks_ref[k]
        near_values = product(far_ref, far, block, 1)
        far_values = product(near_ref, near, block, 0)
        near_values = jnp.where(far_half == 0, near_values[:nv], near_values[nv:])
        far_values = jnp.where(near_half == 0, far_values[:nv], far_values[nv:])
        near_out[near_chunk, near_half] += jnp.where(k < live, near_values, 0.0)
        far_out[far_chunk, far_half] += jnp.where(k < live, far_values, 0.0)


def first_kernel(
    lists_ref, near_ref, far_ref, blocks_ref, near_out, far_out, near_sums, far_sums
):
    place_products(lists_ref, near_ref, far_ref, blocks_ref, near_sums, far_sums)
    for out_ref, sums_ref in ((near_out, near_sums), (far_out, far_sums)):
        for n in range(out_ref.shape[0]):
            out_ref[n] = jnp.concatenate([sums_ref[n, 0], sums_ref[n, 1]], axis=0).astype(BF16)


def second_kernel(
    lists_ref,
    near_ref,
    far_ref,
    blocks_ref,
    state_ref,
    out_ref,
    far_out,
    sums_ref,
):
    place_products(lists_ref, near_ref, far_ref, blocks_ref, sums_ref, far_out)
    nv, width = sums_ref.shape[2:]
    total = jnp.zeros((4 * nv, 4 * nv), F32)
    for n in range(out_ref.shape[0]):
        pair = jnp.concatenate([sums_ref[n, 0], sums_ref[n, 1]], axis=0)
        high, low = split_two(pair)
        total = total + lax.dot_general(
            jnp.concatenate([high, low], axis=0),
            near_ref[n],
            (((1,), (1,)), ((), ())),
            preferred_element_type=F32,
        )
    total = total[: 2 * nv] + total[2 * nv :]
    total = total[:, : 2 * nv] + total[:, 2 * nv :]
    quadratic = total[:nv, :nv] + total[nv:, nv:]
    quadratic = quadratic + contract_last(identity(nv), quadratic)
    shifted = state_ref[nv : 2 * nv]
    quadratic = quadratic + contract_last(shifted, state_ref[3 * nv : 4 * nv] * shifted)
    extra = pack_extra(jnp.concatenate([state_ref[4 * nv :, : 5 * nv], quadratic], axis=1))
    for n in range(out_ref.shape[0]):
        out_ref[n] = jnp.concatenate([sums_ref[n, 0], sums_ref[n, 1], extra], axis=0).astype(BF16)


def middle_kernel(near_ref, far_ref, constants_ref, state_ref, payload_ref):
    nv, width = near_ref.shape[1] // 2, near_ref.shape[2]
    off = jnp.sum(near_ref[...].astype(F32), axis=0) + jnp.sum(far_ref[...].astype(F32), axis=0)
    total = jnp.zeros((3 * nv, 3 * nv), F32)
    halves = []
    for t in range(2):
        part = slice(t * width, (t + 1) * width)
        current = constants_ref[:nv, part]
        diag = constants_ref[2 * nv :, part]
        applied = off[t * nv : (t + 1) * nv] + diag * current
        shifted = applied - constants_ref[nv : 2 * nv, part] - SHIFT * current
        stack = jnp.concatenate([current, shifted, applied], axis=0)
        state_ref[: 3 * nv, part] = stack
        state_ref[3 * nv : 4 * nv, part] = diag
        total = total + contract_last(stack, stack)
        halves.append(shifted)
    pair = jnp.concatenate(halves, axis=0)
    high = pair.astype(BF16).astype(F32)
    chunk = jnp.concatenate([high, pair - high], axis=0).astype(BF16)
    payload_ref[...] = jnp.broadcast_to(chunk[None], payload_ref.shape)
    state_ref[4 * nv :] = jnp.concatenate(
        [
            total[:nv, :nv],
            total[nv : 2 * nv, nv : 2 * nv],
            total[:nv, nv : 2 * nv],
            total[nv : 2 * nv, 2 * nv :],
            total[:nv, 2 * nv :],
            jnp.zeros((nv, 2 * width - 5 * nv), F32),
        ],
        axis=1,
    )


def forward_kernel(near_ref, far_ref, state_ref, late_ref, out_ref):
    nv = far_ref.shape[2]
    width = far_ref.shape[3]
    total = jnp.sum(near_ref[...].astype(F32), axis=0)
    late_ref[: 3 * nv] = state_ref[: 3 * nv]
    for t in range(2):
        part = slice(t * width, (t + 1) * width)
        late_ref[3 * nv :, part] = (
            total[t * nv : (t + 1) * nv] + state_ref[3 * nv : 4 * nv, part] * state_ref[nv : 2 * nv, part]
        )
    extra = pack_extra(unpack_extra(total[2 * nv :]))
    for n in range(out_ref.shape[0]):
        out_ref[n] = jnp.concatenate([far_ref[n, 0], far_ref[n, 1], extra], axis=0).astype(BF16)


def last_kernel(rows_total, far_ref, state_ref, residual_ref, next_ref, coefficients_ref):
    nv, width = coefficients_ref.shape[1], far_ref.shape[2]
    received = jnp.sum(far_ref[...].astype(F32), axis=0)
    extra = unpack_extra(received[2 * nv :])
    gram = lambda i: extra[:, i * nv : (i + 1) * nv]
    cc, xx, cx, xu, cu, xw = (gram(i) for i in range(6))
    eye = identity(nv)
    xc = transposed(cx)
    scale = 1.0 / rows_total
    alpha_one = (cx + SHIFT * cc) * scale
    alpha = alpha_one - SHIFT * eye
    alpha_t = (xc + SHIFT * cc) * scale - SHIFT * eye
    adjusted_c = xc - small_dot(alpha_t, cc)
    work = (xx - small_dot(alpha_t, cx) - small_dot(adjusted_c, alpha)) * scale
    rows = lax.broadcasted_iota(jnp.int32, (nv, nv), 0)
    columns = lax.broadcasted_iota(jnp.int32, (nv, nv), 1)
    factor = jnp.zeros((nv, nv), F32)
    factor_t = jnp.zeros((nv, nv), F32)
    inverse = eye
    inverse_t = eye
    for j in range(nv):
        root = lax.rsqrt(work[j : j + 1, j : j + 1])
        column = jnp.where(rows[:, :1] >= j, work[:, j : j + 1] * root, 0.0)
        row = jnp.where(columns[:1] >= j, work[j : j + 1, :] * root, 0.0)
        factor = jnp.where(columns == j, column, factor)
        factor_t = jnp.where(rows == j, row, factor_t)
        work = work - column * row
        done = inverse[j : j + 1, :] * root
        below = jnp.where(rows[:, :1] > j, column, 0.0)
        inverse = jnp.where(rows == j, done, inverse - below * done)
        done_t = inverse_t[:, j : j + 1] * root
        right = jnp.where(columns[:1] > j, row, 0.0)
        inverse_t = jnp.where(columns == j, done_t, inverse_t - done_t * right)
    half = small_dot(xu, alpha)
    z = (
        xw
        - half
        - transposed(half)
        + small_dot(small_dot(alpha_t, cu), alpha)
    )
    alpha_two = small_dot(small_dot(inverse, z), inverse_t)
    alpha_two = (alpha_two - small_dot(small_dot(inverse, adjusted_c), factor)) * scale
    alpha_two_t = transposed(alpha_two)
    for t in range(2):
        part = slice(t * width, (t + 1) * width)
        current = state_ref[:nv, part]
        shifted = state_ref[nv : 2 * nv, part]
        applied = state_ref[2 * nv : 3 * nv, part]
        applied_shifted = state_ref[3 * nv :, part] + received[t * nv : (t + 1) * nv]
        following = small_dot(inverse, shifted - small_dot(alpha_t, current))
        second = small_dot(inverse, applied_shifted - small_dot(alpha_t, applied))
        second = second - small_dot(factor_t, current)
        next_ref[:, part] = following
        residual_ref[:, part] = second - small_dot(alpha_two_t, following)
    coefficients_ref[0] = alpha_one
    coefficients_ref[1] = factor
    coefficients_ref[2] = alpha_two


def on_device(
    current_block, previous_block, beta_coupling, diagonal, blocks, near_index, far_index, counts
):
    tile_blocks = blocks[0, 0]
    lists = jnp.concatenate([near_index[0, 0], far_index[0, 0], counts[0]])
    nv, share = current_block.shape
    width = tile_blocks.shape[1]
    n_row, n_col = lax.axis_size("row"), lax.axis_size("col")
    rows_total = share * n_row * n_col
    near_sums, far_sums = (n_col, 2, nv, width), (n_row, 2, nv, width)

    chunks = call(rounded_kernel, shape_of((n_col, 2 * nv, width), BF16), [VMEM])(current_block)
    constants, held_blocks = call(
        pack_kernel, (shape_of((3 * nv, share)), shape_of(tile_blocks.shape, BF16)), [VMEM] * 5
    )(current_block, previous_block, beta_coupling, diagonal.reshape(1, share), tile_blocks)
    near_vectors = exchange(chunks, "col")
    far_vectors = exchange(chunks, "row")
    near_part, far_part = call(
        first_kernel,
        (shape_of((n_col, 2 * nv, width), BF16), shape_of((n_row, 2 * nv, width), BF16)),
        [SMEM, VMEM, VMEM, VMEM],
        [pltpu.VMEM(near_sums, F32), pltpu.VMEM(far_sums, F32)],
    )(lists, near_vectors, far_vectors, held_blocks)
    far_got = exchange(far_part, "row")
    near_got = exchange(near_part, "col")
    state, chunks = call(
        middle_kernel,
        (shape_of((5 * nv, share)), shape_of((n_col, 4 * nv, width), BF16)),
        [VMEM] * 3,
    )(near_got, far_got, constants)

    far_vectors = exchange(chunks, "row")
    near_vectors = exchange(chunks, "col")
    near_part, far_part = call(
        second_kernel,
        (shape_of((n_col, 3 * nv, width), BF16), shape_of(far_sums)),
        [SMEM, VMEM, VMEM, VMEM, VMEM],
        [pltpu.VMEM(near_sums, F32)],
    )(lists, near_vectors, far_vectors, held_blocks, state)
    near_got = exchange(near_part, "col")
    late, far_part = call(
        forward_kernel,
        (shape_of((4 * nv, share)), shape_of((n_row, 3 * nv, width), BF16)),
        [VMEM] * 3,
    )(near_got, far_part, state)
    far_got = exchange(far_part, "row")
    return call(
        functools.partial(last_kernel, rows_total),
        (shape_of((nv, share)), shape_of((nv, share)), shape_of((3, nv, nv))),
        [VMEM] * 2,
    )(far_got, late)


def solution(mesh):
    return jax.shard_map(
        on_device,
        mesh=mesh,
        in_specs=(
            P(None, ("row", "col")),
            P(None, ("row", "col")),
            P(),
            P(("row", "col")),
            P("row", "col", None, None, None),
            P("row", "col", None),
            P("row", "col", None),
            P("row", "col"),
        ),
        out_specs=(P(None, ("row", "col")), P(None, ("row", "col")), P()),
        check_vma=False,
    )
```

```python
import functools

import jax
import jax.numpy as jnp
from jax import lax
from jax.experimental import pallas as pl
from jax.experimental.pallas import tpu as pltpu
from jax.sharding import PartitionSpec as P

HIGHEST = lax.Precision.HIGHEST
F32 = jnp.float32
BF16 = jnp.bfloat16
SHIFT = 1.25
VMEM = pl.BlockSpec(memory_space=pltpu.VMEM)
SMEM = pl.BlockSpec(memory_space=pltpu.SMEM)
PARAMS = pltpu.CompilerParams(vmem_limit_bytes=24 * 1024 * 1024)


def exchange(chunks, axis):
    return lax.all_to_all(chunks, axis, split_axis=0, concat_axis=0, tiled=True)


def call(kernel, out_shape, in_specs, scratch=()):
    many = isinstance(out_shape, (list, tuple))
    return pl.pallas_call(
        kernel,
        out_shape=out_shape,
        in_specs=in_specs,
        out_specs=tuple(VMEM for _ in out_shape) if many else VMEM,
        scratch_shapes=list(scratch),
        compiler_params=PARAMS,
    )


def shape_of(shape, dtype=F32):
    return jax.ShapeDtypeStruct(shape, dtype)


def pieces(ref):
    width = ref.shape[-1] // 2
    return [ref[:, :width], ref[:, width:]]


def contract_last(left, right):
    return lax.dot_general(
        left, right, (((1,), (1,)), ((), ())), precision=HIGHEST, preferred_element_type=F32
    )


def small_dot(left, right):
    total = left[:, 0:1] * right[0:1, :]
    for k in range(1, right.shape[0]):
        total = total + left[:, k : k + 1] * right[k : k + 1, :]
    return total


def transposed(matrix):
    size = matrix.shape[0]
    tile = jnp.concatenate([matrix, jnp.zeros((size, 128 - size), F32)], axis=1)
    return jnp.transpose(tile)[:size]


def identity(size):
    rows = lax.broadcasted_iota(jnp.int32, (size, size), 0)
    return (rows == lax.broadcasted_iota(jnp.int32, (size, size), 1)).astype(F32)


def split_two(values):
    high = values.astype(BF16)
    return high, (values - high.astype(F32)).astype(BF16)


def pack_extra(extra):
    high = extra.astype(BF16).astype(F32)
    rest = extra - high
    middle = rest.astype(BF16).astype(F32)
    low = rest - middle
    nv = extra.shape[0]
    return jnp.concatenate([high, middle, low[:, : 4 * nv]], axis=1)


def unpack_extra(total):
    nv = total.shape[0]
    low = jnp.concatenate([total[:, 12 * nv :], jnp.zeros((nv, 2 * nv), F32)], axis=1)
    return total[:, : 6 * nv] + (total[:, 6 * nv : 12 * nv] + low)


def rounded_kernel(vectors_ref, out_ref):
    chunk = jnp.concatenate(pieces(vectors_ref), axis=0).astype(BF16)
    out_ref[...] = jnp.broadcast_to(chunk[None], out_ref.shape)


def pack_kernel(
    current_ref, previous_ref, beta_ref, diagonal_ref, blocks_ref, out_ref, held_ref
):
    nv = current_ref.shape[0]
    held_ref[...] = blocks_ref[...]
    out_ref[:nv] = current_ref[...]
    out_ref[nv : 2 * nv] = small_dot(beta_ref[...], previous_ref[...])
    out_ref[2 * nv :] = jnp.broadcast_to(diagonal_ref[...], (nv, out_ref.shape[1]))


def place_products(lists_ref, near_ref, far_ref, blocks_ref, near_out, far_out):
    slots = blocks_ref.shape[0]
    nv = near_out.shape[2]

    def product(ref, index, block, block_dim):
        pair = ref[lax.shift_right_logical(index, 1)]
        values = lax.dot_general(
            pair, block, (((1,), (block_dim,)), ((), ())), preferred_element_type=F32
        )
        if ref.shape[1] > 2 * nv:
            values = values[: 2 * nv] + values[2 * nv :]
        return values

    near_out[...] = jnp.zeros_like(near_out)
    far_out[...] = jnp.zeros_like(far_out)
    live = lists_ref[2 * slots]
    for k in range(slots):
        near, far = lists_ref[k], lists_ref[slots + k]
        near_half, far_half = near & 1, far & 1
        near_chunk, far_chunk = lax.shift_right_logical(near, 1), lax.shift_right_logical(far, 1)
        block = blocks_ref[k]
        near_values = product(far_ref, far, block, 1)
        far_values = product(near_ref, near, block, 0)
        near_values = jnp.where(far_half == 0, near_values[:nv], near_values[nv:])
        far_values = jnp.where(near_half == 0, far_values[:nv], far_values[nv:])
        near_out[near_chunk, near_half] += jnp.where(k < live, near_values, 0.0)
        far_out[far_chunk, far_half] += jnp.where(k < live, far_values, 0.0)


def first_kernel(
    lists_ref, near_ref, far_ref, blocks_ref, near_out, far_out, near_sums, far_sums
):
    place_products(lists_ref, near_ref, far_ref, blocks_ref, near_sums, far_sums)
    for out_ref, sums_ref in ((near_out, near_sums), (far_out, far_sums)):
        for n in range(out_ref.shape[0]):
            out_ref[n] = jnp.concatenate([sums_ref[n, 0], sums_ref[n, 1]], axis=0).astype(BF16)


def second_kernel(
    lists_ref,
    near_ref,
    far_ref,
    blocks_ref,
    state_ref,
    out_ref,
    far_out,
    sums_ref,
):
    place_products(lists_ref, near_ref, far_ref, blocks_ref, sums_ref, far_out)
    nv, width = sums_ref.shape[2:]
    total = jnp.zeros((4 * nv, 4 * nv), F32)
    for n in range(out_ref.shape[0]):
        pair = jnp.concatenate([sums_ref[n, 0], sums_ref[n, 1]], axis=0)
        high, low = split_two(pair)
        total = total + lax.dot_general(
            jnp.concatenate([high, low], axis=0),
            near_ref[n],
            (((1,), (1,)), ((), ())),
            preferred_element_type=F32,
        )
    total = total[: 2 * nv] + total[2 * nv :]
    total = total[:, : 2 * nv] + total[:, 2 * nv :]
    quadratic = total[:nv, :nv] + total[nv:, nv:]
    quadratic = quadratic + contract_last(identity(nv), quadratic)
    shifted = state_ref[nv : 2 * nv]
    quadratic = quadratic + contract_last(shifted, state_ref[3 * nv : 4 * nv] * shifted)
    extra = pack_extra(jnp.concatenate([state_ref[4 * nv :, : 5 * nv], quadratic], axis=1))
    for n in range(out_ref.shape[0]):
        out_ref[n] = jnp.concatenate([sums_ref[n, 0], sums_ref[n, 1], extra], axis=0).astype(BF16)


def middle_kernel(near_ref, far_ref, constants_ref, state_ref, payload_ref):
    nv, width = near_ref.shape[1] // 2, near_ref.shape[2]
    off = jnp.sum(near_ref[...].astype(F32), axis=0) + jnp.sum(far_ref[...].astype(F32), axis=0)
    total = jnp.zeros((3 * nv, 3 * nv), F32)
    halves = []
    for t in range(2):
        part = slice(t * width, (t + 1) * width)
        current = constants_ref[:nv, part]
        diag = constants_ref[2 * nv :, part]
        applied = off[t * nv : (t + 1) * nv] + diag * current
        shifted = applied - constants_ref[nv : 2 * nv, part] - SHIFT * current
        stack = jnp.concatenate([current, shifted, applied], axis=0)
        state_ref[: 3 * nv, part] = stack
        state_ref[3 * nv : 4 * nv, part] = diag
        total = total + contract_last(stack, stack)
        halves.append(shifted)
    pair = jnp.concatenate(halves, axis=0)
    high = pair.astype(BF16).astype(F32)
    chunk = jnp.concatenate([high, pair - high], axis=0).astype(BF16)
    payload_ref[...] = jnp.broadcast_to(chunk[None], payload_ref.shape)
    state_ref[4 * nv :] = jnp.concatenate(
        [
            total[:nv, :nv],
            total[nv : 2 * nv, nv : 2 * nv],
            total[:nv, nv : 2 * nv],
            total[nv : 2 * nv, 2 * nv :],
            total[:nv, 2 * nv :],
            jnp.zeros((nv, 2 * width - 5 * nv), F32),
        ],
        axis=1,
    )


def forward_kernel(near_ref, far_ref, state_ref, late_ref, out_ref):
    nv = far_ref.shape[2]
    width = far_ref.shape[3]
    total = jnp.sum(near_ref[...].astype(F32), axis=0)
    late_ref[: 3 * nv] = state_ref[: 3 * nv]
    for t in range(2):
        part = slice(t * width, (t + 1) * width)
        late_ref[3 * nv :, part] = (
            total[t * nv : (t + 1) * nv] + state_ref[3 * nv : 4 * nv, part] * state_ref[nv : 2 * nv, part]
        )
    extra = pack_extra(unpack_extra(total[2 * nv :]))
    for n in range(out_ref.shape[0]):
        out_ref[n] = jnp.concatenate([far_ref[n, 0], far_ref[n, 1], extra], axis=0).astype(BF16)


def last_kernel(rows_total, far_ref, state_ref, residual_ref, next_ref, coefficients_ref):
    nv, width = coefficients_ref.shape[1], far_ref.shape[2]
    received = jnp.sum(far_ref[...].astype(F32), axis=0)
    extra = unpack_extra(received[2 * nv :])
    gram = lambda i: extra[:, i * nv : (i + 1) * nv]
    cc, xx, cx, xu, cu, xw = (gram(i) for i in range(6))
    eye = identity(nv)
    xc = transposed(cx)
    scale = 1.0 / rows_total
    alpha_one = (cx + SHIFT * cc) * scale
    alpha = alpha_one - SHIFT * eye
    alpha_t = (xc + SHIFT * cc) * scale - SHIFT * eye
    adjusted_c = xc - small_dot(alpha_t, cc)
    work = (xx - small_dot(alpha_t, cx) - small_dot(adjusted_c, alpha)) * scale
    rows = lax.broadcasted_iota(jnp.int32, (nv, nv), 0)
    columns = lax.broadcasted_iota(jnp.int32, (nv, nv), 1)
    factor = jnp.zeros((nv, nv), F32)
    factor_t = jnp.zeros((nv, nv), F32)
    inverse = eye
    inverse_t = eye
    for j in range(nv):
        root = lax.rsqrt(work[j : j + 1, j : j + 1])
        column = jnp.where(rows[:, :1] >= j, work[:, j : j + 1] * root, 0.0)
        row = jnp.where(columns[:1] >= j, work[j : j + 1, :] * root, 0.0)
        factor = jnp.where(columns == j, column, factor)
        factor_t = jnp.where(rows == j, row, factor_t)
        work = work - column * row
        done = inverse[j : j + 1, :] * root
        below = jnp.where(rows[:, :1] > j, column, 0.0)
        inverse = jnp.where(rows == j, done, inverse - below * done)
        done_t = inverse_t[:, j : j + 1] * root
        right = jnp.where(columns[:1] > j, row, 0.0)
        inverse_t = jnp.where(columns == j, done_t, inverse_t - done_t * right)
    half = small_dot(xu, alpha)
    z = (
        xw
        - half
        - transposed(half)
        + small_dot(small_dot(alpha_t, cu), alpha)
    )
    alpha_two = small_dot(small_dot(inverse, z), inverse_t)
    alpha_two = (alpha_two - small_dot(small_dot(inverse, adjusted_c), factor)) * scale
    alpha_two_t = transposed(alpha_two)
    for t in range(2):
        part = slice(t * width, (t + 1) * width)
        current = state_ref[:nv, part]
        shifted = state_ref[nv : 2 * nv, part]
        applied = state_ref[2 * nv : 3 * nv, part]
        applied_shifted = state_ref[3 * nv :, part] + received[t * nv : (t + 1) * nv]
        following = small_dot(inverse, shifted - small_dot(alpha_t, current))
        second = small_dot(inverse, applied_shifted - small_dot(alpha_t, applied))
        second = second - small_dot(factor_t, current)
        next_ref[:, part] = following
        residual_ref[:, part] = second - small_dot(alpha_two_t, following)
    coefficients_ref[0] = alpha_one
    coefficients_ref[1] = factor
    coefficients_ref[2] = alpha_two


def on_device(
    current_block, previous_block, beta_coupling, diagonal, blocks, near_index, far_index, counts
):
    tile_blocks = blocks[0, 0]
    lists = jnp.concatenate([near_index[0, 0], far_index[0, 0], counts[0]])
    nv, share = current_block.shape
    width = tile_blocks.shape[1]
    n_row, n_col = lax.axis_size("row"), lax.axis_size("col")
    rows_total = share * n_row * n_col
    near_sums, far_sums = (n_col, 2, nv, width), (n_row, 2, nv, width)

    chunks = call(rounded_kernel, shape_of((n_col, 2 * nv, width), BF16), [VMEM])(current_block)
    constants, held_blocks = call(
        pack_kernel, (shape_of((3 * nv, share)), shape_of(tile_blocks.shape, BF16)), [VMEM] * 5
    )(current_block, previous_block, beta_coupling, diagonal.reshape(1, share), tile_blocks)
    near_vectors = exchange(chunks, "col")
    far_vectors = exchange(chunks, "row")
    near_part, far_part = call(
        first_kernel,
        (shape_of((n_col, 2 * nv, width), BF16), shape_of((n_row, 2 * nv, width), BF16)),
        [SMEM, VMEM, VMEM, VMEM],
        [pltpu.VMEM(near_sums, F32), pltpu.VMEM(far_sums, F32)],
    )(lists, near_vectors, far_vectors, held_blocks)
    far_got = exchange(far_part, "row")
    near_got = exchange(near_part, "col")
    state, chunks = call(
        middle_kernel,
        (shape_of((5 * nv, share)), shape_of((n_col, 4 * nv, width), BF16)),
        [VMEM] * 3,
    )(near_got, far_got, constants)

    near_vectors = exchange(chunks, "col")
    chunks, near_vectors = lax.optimization_barrier((chunks, near_vectors))
    far_vectors = exchange(chunks, "row")
    near_part, far_part = call(
        second_kernel,
        (shape_of((n_col, 3 * nv, width), BF16), shape_of(far_sums)),
        [SMEM, VMEM, VMEM, VMEM, VMEM],
        [pltpu.VMEM(near_sums, F32)],
    )(lists, near_vectors, far_vectors, held_blocks, state)
    near_got = exchange(near_part, "col")
    late, far_part = call(
        forward_kernel,
        (shape_of((4 * nv, share)), shape_of((n_row, 3 * nv, width), BF16)),
        [VMEM] * 3,
    )(near_got, far_part, state)
    far_got = exchange(far_part, "row")
    return call(
        functools.partial(last_kernel, rows_total),
        (shape_of((nv, share)), shape_of((nv, share)), shape_of((3, nv, nv))),
        [VMEM] * 2,
    )(far_got, late)


def solution(mesh):
    return jax.shard_map(
        on_device,
        mesh=mesh,
        in_specs=(
            P(None, ("row", "col")),
            P(None, ("row", "col")),
            P(),
            P(("row", "col")),
            P("row", "col", None, None, None),
            P("row", "col", None),
            P("row", "col", None),
            P("row", "col"),
        ),
        out_specs=(P(None, ("row", "col")), P(None, ("row", "col")), P()),
        check_vma=False,
    )
```
